256 devices in a mesh: inner: 8 (over x_hi, y), outer: 8 (over z), dp: 4 (over x_lo, core).
Axes of the slice: x: 4 (x_hi: 2, x_lo: 2; x = x_hi * 2 + x_lo), y: 4, z: 8, core: 2. Of those that a mesh axis runs over, the one named last changes fastest.
Arguments:
- queries: bfloat16 [4, 8192, 1024], P('dp', ('inner', 'outer')), may hold values from -8 to 8
- key_states: bfloat16 [4, 8192, 1024], P('dp', ('inner', 'outer')), may hold values from -8 to 8
- value_states: bfloat16 [4, 8192, 1024], P('dp', ('inner', 'outer')), may hold values from -6 to 6
- attention: bfloat16 [4, 8192, 1024], P('dp', ('inner', 'outer')), may hold values from -6 to 6
- row_lse: float32 [4, 8192, 8], P('dp', ('inner', 'outer')), may hold values from 0 to 64, as said below
- grad_output: bfloat16 [4, 8192, 3072], P('dp', ('inner', 'outer')), may hold values from -16 to 16
- out_weight: bfloat16 [3072, 1024], replicated, may hold values from -0.109375 to 0.109375
- pad_counts: int32 [4, 64], P('dp', ('inner', 'outer')), may hold values from 0 to 63
Outputs:
- grad_query: bfloat16 [4, 8192, 1024], P('dp', ('inner', 'outer'))
- grad_key: bfloat16 [4, 8192, 1024], P('dp', ('inner', 'outer'))
- grad_value: bfloat16 [4, 8192, 1024], P('dp', ('inner', 'outer'))
- weight_grad: float32 [3072, 1024], P(('inner', 'outer', 'dp'))
The draws below stay inside these ranges and needn't reach their ends.
Inputs may be any that keep to these rules, and one draw needn't show every extreme that they name: `row_lse`: each entry is the logarithm of the sum, over that query's valid keys, of exp(scores) in that head, for the given queries, key_states and pad_counts.
All inputs are finite; a program needn't handle non-finite values.
Results may differ from the reference program's by a relative error of at most 0.023.
Values may be sent and summed in bfloat16 or wider, within the bound.
No kernel may reach another device: no remote copies, remote signals or barrier semaphores. Data moves between devices by JAX's collectives and lax.ppermute only.
A program may use at most 128 MiB of HBM per device.

```python
import math
import jax
import jax.numpy as jnp
from jax import lax

D = 3072
HEADS = 8
HEAD = 128
TOK_DEV = 128
HD = 1024
TOKENS = 8192
REPLICAS = 4


def query_key_pair(key, spread):
    strength = jnp.exp(jax.random.uniform(jax.random.fold_in(key, 101), (REPLICAS, HEADS), jnp.float32, 0.0, math.log(5.0)))
    amplitude = jnp.repeat(jnp.sqrt(strength), HEAD, axis=1)[:, None, :]
    shape = (REPLICAS, TOKENS, HD)
    query_drawn = jnp.clip(jax.random.normal(jax.random.fold_in(key, 102), shape, jnp.float32), -3.5, 3.5)
    key_drawn = jnp.clip(jax.random.normal(jax.random.fold_in(key, 103), shape, jnp.float32), -3.5, 3.5)
    row_scale = jnp.exp(jax.random.uniform(jax.random.fold_in(key, 106), (REPLICAS, TOKENS, 1), jnp.float32, -spread, spread))
    query_mix = query_drawn
    key_mix = key_drawn
    query_low = (query_mix * amplitude * row_scale).astype(jnp.bfloat16)
    key_low = (key_mix * amplitude).astype(jnp.bfloat16)
    return (query_low, key_low)


def padding_counts(key):
    shard_count = TOKENS // TOK_DEV
    total = REPLICAS * shard_count
    base = jax.random.randint(jax.random.fold_in(key, 201), (total,), 0, TOK_DEV // 2)
    first = jax.random.randint(jax.random.fold_in(key, 202), (), 0, total)
    offset = jax.random.randint(jax.random.fold_in(key, 203), (), 1, total)
    second = (first + offset) % total
    places = jnp.arange(total, dtype=jnp.int32)
    base = jnp.where(places == first, TOK_DEV // 2 - 1, base)
    base = jnp.where(places == second, 0, base)
    return base.reshape(REPLICAS, shard_count).astype(jnp.int32)


def head_total(items):
    query_rows, key_rows, valid_keys = items
    width_block = min(1024, TOKENS)
    blocks_count = TOKENS // width_block

    def step(carry, pieces):
        top, total = carry
        block_key, block_valid = pieces
        scores = jnp.dot(query_rows, block_key.T, precision=lax.Precision.HIGHEST) * HEAD ** (-0.5)
        masked = jnp.where(block_valid[None, :], scores, -1e+30)
        new_top = jnp.maximum(top, jnp.max(masked, axis=1))
        total = total * jnp.exp(top - new_top) + jnp.sum(jnp.exp(masked - new_top[:, None]), axis=1)
        return ((new_top, total), None)
    start = (jnp.full((TOKENS,), -1e+30, jnp.float32), jnp.zeros((TOKENS,), jnp.float32))
    blocked = (key_rows.reshape(blocks_count, width_block, HEAD), valid_keys.reshape(blocks_count, width_block))
    (top, total), unused = lax.scan(step, start, blocked)
    return top + jnp.log(total)


def draw_queries(key, part):
    spread = 0.0
    query_low, key_low = query_key_pair(key, spread)
    return query_low


def draw_key_states(key, part):
    spread = 0.0
    query_low, key_low = query_key_pair(key, spread)
    return key_low


def draw_pad_counts(key, part):
    return padding_counts(key)


def draw_row_lse(key, part):
    spread = 0.0
    query_low, key_low = query_key_pair(key, spread)
    pads = padding_counts(key)
    positions = jnp.arange(TOKENS, dtype=jnp.int32)
    valid = (positions % TOK_DEV)[None, :] < TOK_DEV - pads[:, positions // TOK_DEV]
    query_heads = query_low.astype(jnp.float32).reshape(REPLICAS, TOKENS, HEADS, HEAD)
    query_heads = query_heads.transpose(0, 2, 1, 3).reshape(REPLICAS * HEADS, TOKENS, HEAD)
    key_heads = key_low.astype(jnp.float32).reshape(REPLICAS, TOKENS, HEADS, HEAD)
    key_heads = key_heads.transpose(0, 2, 1, 3).reshape(REPLICAS * HEADS, TOKENS, HEAD)
    valid_heads = jnp.repeat(valid, HEADS, axis=0)
    totals = lax.map(head_total, (query_heads, key_heads, valid_heads))
    return totals.reshape(REPLICAS, HEADS, TOKENS).transpose(0, 2, 1).astype(jnp.float32)


def strengthened(values, stream_key, source, target, blocks, factor):
    owner, partner = [(jnp.arange(values.shape[axis_at]) // (values.shape[axis_at] // blocks)).reshape([-1 if axis == axis_at else 1 for axis in range(values.ndim)]) for axis_at in (source, target)]
    chosen = jax.random.permutation(stream_key, blocks)[partner]
    strong = (owner == chosen) | (owner == (partner + blocks // 2) % blocks)
    return jnp.where(strong, factor * values, values)


def levels(key, dims, cuts, low, high):
    def one(axis_at, blocks):
        heights = jax.random.uniform(jax.random.fold_in(jax.random.fold_in(key, 6), axis_at), (blocks,), jnp.float32, low / len(cuts), high / len(cuts))
        return jnp.repeat(jnp.exp(heights), dims[axis_at] // blocks).reshape((-1,) + (1,) * (len(dims) - axis_at - 1))

    loudness = one(*cuts[0])
    for cut in cuts[1:]:
        loudness = loudness * one(*cut)
    return loudness


def scatter_about(key, dims, deviation, reach, shards=(), kind=jnp.bfloat16):
    factor_of = levels(key, dims, shards, -0.22, 0.18) if shards else 1.0
    values = jax.random.normal(key, dims, jnp.float32) * deviation * factor_of
    return jnp.minimum(jnp.maximum(values, -reach), reach).astype(kind)


def heavy_noise(own_key, shape, scale, most, cuts, heavy, held_as=jnp.bfloat16):
    drawn = scale * jax.random.normal(own_key, shape, jnp.float32)
    if cuts:
        drawn = drawn * levels(own_key, shape, cuts, -0.22, 0.18)
    return jnp.clip(strengthened(drawn, jax.random.fold_in(own_key, 3), *heavy), -most, most).astype(held_as)


def setup_inputs(seed: int = 0) -> dict:
    seeds = jax.random.split(jax.random.key(seed), 9)
    queries = draw_queries(jax.random.fold_in(seeds[8], 71), 0)
    key_states = draw_key_states(jax.random.fold_in(seeds[8], 71), 0)
    value_states = scatter_about(seeds[2], (REPLICAS, TOKENS, HD), 1.0, 6.0, ((0, 4), (1, 64)))
    attention = scatter_about(seeds[3], (REPLICAS, TOKENS, HD), 1.0, 6.0, ((0, 4), (1, 64)))
    row_lse = draw_row_lse(jax.random.fold_in(seeds[8], 71), 0)
    grad_output = heavy_noise(seeds[5], (REPLICAS, TOKENS, D), 1.0, 16.0, ((0, 4), (1, 64)), (1, 2, 64, 4.0))
    out_weight = scatter_about(seeds[6], (D, HD), D ** -0.5, 0.109375)
    pad_counts = draw_pad_counts(jax.random.fold_in(seeds[8], 71), 0)
    return {"queries": queries, "key_states": key_states, "value_states": value_states, "attention": attention, "row_lse": row_lse, "grad_output": grad_output, "out_weight": out_weight, "pad_counts": pad_counts}


def head_backward(items, keep_mask):
    head_query, head_key, head_value, head_out, head_grad, head_lse = items
    scaling = HEAD ** -0.5
    width_block = min(1024, TOKENS)
    blocks_count = TOKENS // width_block
    delta_rows = jnp.sum(head_grad.astype(jnp.float32) * head_out.astype(jnp.float32), axis=1)
    lse_rows = head_lse.astype(jnp.float32)

    def key_block(query_sum, pieces):
        block_key, block_value, block_keep = pieces
        scores = jnp.dot(head_query, block_key.T, preferred_element_type=jnp.float32) * scaling
        probs = jnp.exp(scores - lse_rows[:, None]) * block_keep[None, :]
        probs_low = probs.astype(jnp.bfloat16)
        value_part = jnp.dot(probs_low.T, head_grad, preferred_element_type=jnp.float32)
        grad_probs = jnp.dot(head_grad, block_value.T, preferred_element_type=jnp.float32)
        grad_scores = (probs * (grad_probs - delta_rows[:, None])).astype(jnp.bfloat16)
        query_sum = query_sum + jnp.dot(grad_scores, block_key, preferred_element_type=jnp.float32) * scaling
        key_part = jnp.dot(grad_scores.T, head_query, preferred_element_type=jnp.float32) * scaling
        return query_sum, (key_part, value_part)

    blocked = (head_key.reshape(blocks_count, width_block, HEAD),
               head_value.reshape(blocks_count, width_block, HEAD),
               keep_mask.reshape(blocks_count, width_block))
    query_sum, parts = lax.scan(key_block, jnp.zeros((TOKENS, HEAD), jnp.float32), blocked)
    key_total = parts[0].reshape(TOKENS, HEAD)
    value_total = parts[1].reshape(TOKENS, HEAD)
    return (query_sum.astype(jnp.bfloat16), key_total.astype(jnp.bfloat16), value_total.astype(jnp.bfloat16))


def to_heads(matrix):
    return matrix.reshape(TOKENS, HEADS, HEAD).transpose(1, 0, 2)


def from_heads(stacked):
    return stacked.transpose(1, 0, 2).reshape(TOKENS, HEADS * HEAD)


def reference(queries, key_states, value_states, attention, row_lse, grad_output, out_weight, pad_counts):
    positions = jnp.arange(TOKENS, dtype=jnp.int32)
    owner_index = positions // TOK_DEV
    within_shard = positions % TOK_DEV

    def replica_backward(items):
        rep_query, rep_key, rep_value, rep_out, rep_lse, rep_grad, rep_pad = items
        grad_attn = jnp.dot(rep_grad, out_weight, preferred_element_type=jnp.float32).astype(jnp.bfloat16)
        keep_mask = (within_shard < TOK_DEV - rep_pad[owner_index]).astype(jnp.float32)
        per_head = (to_heads(rep_query), to_heads(rep_key), to_heads(rep_value), to_heads(rep_out),
                    to_heads(grad_attn), rep_lse.T)
        results = lax.map(lambda pieces: head_backward(pieces, keep_mask), per_head)
        return (from_heads(results[0]), from_heads(results[1]), from_heads(results[2]))

    grads = lax.map(replica_backward, (queries, key_states, value_states, attention, row_lse, grad_output, pad_counts))
    weight_grad = jnp.dot(grad_output.reshape(-1, D).T, attention.reshape(-1, HEADS * HEAD),
                          preferred_element_type=jnp.float32)
    return grads[0], grads[1], grads[2], weight_grad
```

```python
import functools

import jax
import jax.numpy as jnp
from jax import lax
from jax.experimental import pallas as pl
from jax.experimental.pallas import tpu as pltpu
from jax.sharding import PartitionSpec as P

LOG2E = 1.4426950408889634
HEADS = 8
HEAD = 128
TOK = 128
SCALE = HEAD**-0.5
MIB = 2**20
BF16 = jnp.bfloat16
F32 = jnp.float32
VMEM = pl.BlockSpec(memory_space=pltpu.VMEM)
SMEM = pl.BlockSpec(memory_space=pltpu.SMEM)
NT = (((1,), (1,)), ((), ()))
TN = (((0,), (0,)), ((), ()))
NN = (((1,), (0,)), ((), ()))


def dot(a, b, dims):
    return lax.dot_general(a, b, dims, preferred_element_type=F32)


def params(mib):
    return pltpu.CompilerParams(vmem_limit_bytes=mib * MIB)


def shape(dims, dtype=BF16):
    return jax.ShapeDtypeStruct(dims, dtype)


def head_lanes(pos, d):
    head = lax.rem(pos[0] + d, HEADS)
    return pl.ds(pl.multiple_of(head * HEAD, HEAD), HEAD)


def pack_keys_body(pos, k, v, grad, att, *outs):
    kv_outs, wg_outs = outs[:8], outs[8:]
    rows = lax.broadcasted_iota(jnp.int32, (TOK, HEAD), 0)
    valid = rows < TOK - pos[5]
    for d in range(8):
        lanes = head_lanes(pos, d)
        key = k[:, lanes].astype(F32)
        kv_outs[d][0:128, :] = jnp.where(valid, key, 0.0).astype(BF16)
        kv_outs[d][128:256, :] = v[:, lanes]
    for d in range(4):
        block = lax.rem(pos[1] + d, 4)
        for x in range(2):
            columns = pl.ds(pl.multiple_of((x * 4 + block) * 384, 128), 384)
            wg_outs[d][:, x * 384 : (x + 1) * 384] = grad[:, columns]
        wg_outs[d][:, 768:1792] = att[...]


def pack_keys(pos, k, v, grad, att):
    return pl.pallas_call(
        pack_keys_body,
        out_shape=(shape((256, 128)),) * 8 + (shape((128, 1792)),) * 4,
        in_specs=[SMEM, VMEM, VMEM, VMEM, VMEM],
        out_specs=(VMEM,) * 12,
        compiler_params=params(32),
        name="pack_keys",
    )(pos, k, v, grad, att)


def three_parts(row):
    hi = row.astype(BF16).astype(F32)
    rest = row - hi
    mid = rest.astype(BF16).astype(F32)
    return hi, mid, rest - mid


def pack_queries_body(steps, pos, q, att, lse, grad, weight, *refs):
    outs, total, low, stats = refs[:8], refs[8], refs[9], refs[10]
    step = pl.program_id(0)
    part = dot(grad[...], weight[...], NN)

    @pl.when(step == 0)
    def _():
        total[...] = part

    @pl.when(step > 0)
    def _():
        total[...] += part

    @pl.when(step == steps - 1)
    def _():
        low[...] = total[...].astype(BF16)
        for h in range(HEADS):
            lanes = slice(h * HEAD, (h + 1) * HEAD)
            both = low[:, lanes].astype(F32) * att[:, lanes].astype(F32)
            stats[h : h + 1, :] = jnp.sum(both.T, axis=0, keepdims=True)
        for d in range(8):
            head = lax.rem(pos[0] + d, HEADS)
            lanes = head_lanes(pos, d)
            outs[d][0:128, :] = q[:, lanes]
            outs[d][128:256, :] = low[:, lanes]
            lse_row = lse[pl.ds(head, 1), :] * LOG2E
            delta_row = stats[pl.ds(head, 1), :]
            rows = three_parts(lse_row) + three_parts(delta_row)
            rows = jnp.concatenate(rows + (jnp.zeros((10, TOK), F32),), axis=0)
            outs[d][256:272, :] = rows.astype(BF16)


def pack_queries(pos, q, att, lse, grad, weight):
    width = weight.shape[0]
    steps = 6
    depth = width // steps
    whole = lambda *dims: pl.BlockSpec(dims, lambda k: (0,) * len(dims))
    return pl.pallas_call(
        functools.partial(pack_queries_body, steps),
        grid=(steps,),
        out_shape=(shape((272, 128)),) * 8,
        in_specs=[
            SMEM,
            whole(128, 1024),
            whole(128, 1024),
            whole(8, 128),
            pl.BlockSpec((128, depth), lambda k: (0, k)),
            pl.BlockSpec((depth, 1024), lambda k: (k, 0)),
        ],
        out_specs=(whole(272, 128),) * 8,
        scratch_shapes=[
            pltpu.VMEM((128, 1024), F32),
            pltpu.VMEM((128, 1024), BF16),
            pltpu.VMEM((8, 128), F32),
        ],
        compiler_params=params(32),
        name="pack_queries",
    )(pos, q, att, lse, grad, weight)


def attend_body(blocks, has_acc, has_dq, last_dq, last_acc, *refs):
    refs = list(refs)
    take = lambda n: [refs.pop(0) for _ in range(n)]
    (qg,) = take(1)
    kvs = take(blocks)
    accs = take(blocks) if has_acc else [None] * blocks
    dq_in = take(1)[0] if has_dq else None
    (dq_out,) = take(1)
    outs = take(blocks)
    q = qg[:, 0:128, :].reshape(1024, 128)
    g = qg[:, 128:256, :].reshape(1024, 128)
    rows = [qg[j, 256:272, :].astype(F32) for j in range(8)]
    lse = jnp.concatenate([r[0:1] + r[1:2] + r[2:3] for r in rows], axis=1)
    delta = jnp.concatenate([r[3:4] + r[4:5] + r[5:6] for r in rows], axis=1)
    total = dq_in[...] if has_dq else None
    for n in range(blocks):
        kv, acc, out = kvs[n], accs[n], outs[n]
        for at in range(0, 8, 2):
            span = slice(at, at + 2)
            k = kv[span, 0:128, :].reshape(256, 128)
            v = kv[span, 128:256, :].reshape(256, 128)
            probs = jnp.exp2(dot(k, q, NT) * (SCALE * LOG2E) - lse)
            moved = (probs * (dot(v, g, NT) - delta)).astype(BF16)
            value_part = dot(probs.astype(BF16), g, NN).reshape(2, 128, 128)
            key_part = dot(moved, q, NN).reshape(2, 128, 128)
            if has_acc:
                key_part = key_part + acc[span, 0:128, :]
                value_part = value_part + acc[span, 128:256, :]
            if last_acc:
                key_part = key_part * SCALE
            out[span, 0:128, :] = key_part.astype(out.dtype)
            out[span, 128:256, :] = value_part.astype(out.dtype)
            part = dot(k, moved, TN)
            total = part if total is None else total + part
    if last_dq:
        dq_out[...] = (total.T * SCALE).astype(BF16).reshape(8, 128, 128)
    else:
        dq_out[...] = total


def attend(qg, kvs, accs=None, dq=None, last_dq=False, last_acc=False):
    blocks = len(kvs)
    args = [qg] + list(kvs)
    args += list(accs) if accs is not None else []
    args += [dq] if dq is not None else []
    dq_shape = shape((8, 128, 128)) if last_dq else shape((128, 1024), F32)
    acc_shape = shape((8, 256, 128), BF16 if last_acc else F32)
    return pl.pallas_call(
        functools.partial(attend_body, blocks, accs is not None, dq is not None, last_dq, last_acc),
        out_shape=(dq_shape,) + (acc_shape,) * blocks,
        in_specs=[VMEM] * len(args),
        out_specs=(VMEM,) * (1 + blocks),
        compiler_params=params(40),
        cost_estimate=pl.CostEstimate(
            flops=blocks * 10 * 128 * 1024 * 1024,
            bytes_accessed=blocks * 3 * MIB,
            transcendentals=blocks * 1024 * 1024,
        ),
        name="attend",
    )(*args)


def weight_body(pos, b0, b1, b2, b3, keep, send, total, sorted_rows):
    grad = jnp.concatenate([b[:, 0:768] for b in (b0, b1, b2, b3)], axis=0)
    att = jnp.concatenate([b[:, 768:1792] for b in (b0, b1, b2, b3)], axis=0)
    for at in range(0, 768, 256):
        total[at : at + 256, :] = dot(grad[:, at : at + 256], att, TN)
    total[768:776, :] = jnp.zeros((8, 1024), F32)
    for x in range(2):
        for z in range(8):
            for lo in range(2):
                for core in range(2):
                    row = x * 384 + ((z * 2 + lo) * 2 + core) * 12
                    rows = total[row : row + 16, :].astype(BF16)
                    sorted_rows[core * 4 + lo * 2 + x, z] = rows
    for i in range(2):
        for j in range(2):
            at = (pos[3] + i) % 2 * 2 + (pos[2] + j) % 2
            keep[i, j] = sorted_rows[pos[4] * 4 + at]
            send[i, j] = sorted_rows[(1 - pos[4]) * 4 + at]


def weight_part(pos, blocks):
    return pl.pallas_call(
        weight_body,
        out_shape=(shape((2, 2, 8, 16, 1024)),) * 2,
        in_specs=[SMEM] + [VMEM] * 4,
        out_specs=(VMEM,) * 2,
        scratch_shapes=[pltpu.VMEM((776, 1024), F32), pltpu.VMEM((8, 8, 16, 1024), BF16)],
        compiler_params=params(40),
        cost_estimate=pl.CostEstimate(
            flops=2 * 512 * 768 * 1024, bytes_accessed=4 * MIB, transcendentals=0
        ),
        name="weight_part",
    )(pos, *blocks)


def pack_back_body(pos, acc, other, dq, d1, d2, d3, wg, *outs):
    own = dq[...].T * SCALE
    for d in range(8):
        rows = slice(d * 128, (d + 1) * 128)
        query = own[rows] + d1[d].astype(F32) + d2[d].astype(F32) + d3[d].astype(F32)
        outs[d][0:128, :] = query.astype(BF16)
        key = acc[d, 0:128, :] * SCALE + other[d, 0:128, :].astype(F32)
        outs[d][128:256, :] = key.astype(BF16)
        value = acc[d, 128:256, :] + other[d, 128:256, :].astype(F32)
        outs[d][256:384, :] = value.astype(BF16)
        block = lax.rem(pos[0] + 8 - d, 8)
        for j in range(8):
            outs[d][384 + j * 16 : 400 + j * 16, :] = wg[block, :, j * 128 : (j + 1) * 128]


def pack_back(pos, acc, other, dq, back, wg):
    return pl.pallas_call(
        pack_back_body,
        out_shape=(shape((512, 128)),) * 8,
        in_specs=[SMEM] + [VMEM] * 7,
        out_specs=(VMEM,) * 8,
        compiler_params=params(32),
        name="pack_back",
    )(pos, acc, other, dq, *back, wg)


def unpack_body(pos, *refs):
    ins, (gq, gk, gv, wg) = refs[:8], refs[8:]
    rows = lax.broadcasted_iota(jnp.int32, (TOK, HEAD), 0)
    valid = rows < TOK - pos[5]
    for d in range(8):
        lanes = head_lanes(pos, d)
        gq[:, lanes] = ins[d][0:128, :]
        gk[:, lanes] = jnp.where(valid, ins[d][128:256, :].astype(F32), 0.0).astype(BF16)
        gv[:, lanes] = jnp.where(valid, ins[d][256:384, :].astype(F32), 0.0).astype(BF16)
    for j in range(8):
        span = slice(384 + j * 16, 400 + j * 16)
        total = ins[0][span, :].astype(F32)
        for d in range(1, 8):
            total = total + ins[d][span, :].astype(F32)
        wg[:, j * 128 : (j + 1) * 128] = total[0:12]


def unpack(pos, slots):
    return pl.pallas_call(
        unpack_body,
        out_shape=(shape((128, 1024)),) * 3 + (shape((12, 1024), F32),),
        in_specs=[SMEM] + [VMEM] * 8,
        out_specs=(VMEM,) * 4,
        compiler_params=params(32),
        name="unpack",
    )(pos, *slots)


def z_shift(block, distance):
    return lax.ppermute(block, "outer", [(i, (i + distance) % 8) for i in range(8)])


def y_shift(block, distance):
    route = [(i, i // 4 * 4 + (i + distance) % 4) for i in range(8)]
    return lax.ppermute(block, "inner", route)


def x_swap(block):
    return lax.ppermute(block, "inner", [(i, (i + 4) % 8) for i in range(8)])


def dp_swap(block, bit):
    return lax.ppermute(block, "dp", [(i, i ^ bit) for i in range(4)])


ORDER = (4, 3, 5, 2, 6, 1, 7)


def exchange(slots, sign):
    got = {0: slots[0]}
    for d in ORDER:
        got[d] = z_shift(slots[d], sign * d)
    return [got[d] for d in range(8)]


def on_device(
    queries, key_states, value_states, attention, row_lse, grad_output, out_weight, pad_counts
):
    inner = lax.axis_index("inner")
    dp = lax.axis_index("dp")
    pos = jnp.stack(
        [lax.axis_index("outer"), inner % 4, inner // 4, dp // 2, dp % 2, pad_counts[0, 0]]
    ).astype(jnp.int32)

    packed = pack_keys(pos, key_states[0], value_states[0], grad_output[0], attention[0])
    kv = jnp.stack(exchange(packed[:8], 1))
    q_slots = pack_queries(
        pos, queries[0], attention[0], row_lse[0].T, grad_output[0], out_weight
    )
    qg = jnp.stack(exchange(q_slots, 1))
    kv_far = x_swap(kv)
    qg1, qg3, qg2 = y_shift(qg, 1), y_shift(qg, 3), y_shift(qg, 2)
    wg_blocks = [packed[8]] + [y_shift(packed[8 + d], d) for d in (1, 2, 3)]

    keep, send = weight_part(pos, wg_blocks)
    came = dp_swap(send, 1)
    out_lo = (keep[1].astype(F32) + came[1].astype(F32)).astype(BF16)
    half = keep[0].astype(F32) + came[0].astype(F32) + dp_swap(out_lo, 2).astype(F32)
    wg = (half[0] + x_swap(half[1].astype(BF16)).astype(F32)).astype(BF16)

    dq0, acc = attend(qg, [kv])
    dq0, far = attend(qg, [kv_far], None, dq0)
    dq1, far, acc = attend(qg1, [kv_far, kv], [far, acc], last_dq=True)
    back1 = y_shift(dq1, 3)
    dq3, far, acc = attend(qg3, [kv_far, kv], [far, acc], last_dq=True)
    back3 = y_shift(dq3, 1)
    dq2, far = attend(qg2, [kv_far], [far], last_acc=True)
    other = x_swap(far)
    dq2, acc = attend(qg2, [kv], [acc], dq2, last_dq=True)
    back2 = y_shift(dq2, 2)

    back_slots = pack_back(pos, acc, other, dq0, (back1, back2, back3), wg)
    slots = exchange(back_slots, -1)
    gq, gk, gv, weight_grad = unpack(pos, slots)
    return gq[None], gk[None], gv[None], weight_grad


def solution(mesh):
    tokens = P("dp", ("inner", "outer"), None)
    return jax.shard_map(
        on_device,
        mesh=mesh,
        in_specs=(tokens,) * 6 + (P(), P("dp", ("inner", "outer"))),
        out_specs=(tokens,) * 3 + (P(("inner", "outer", "dp"), None),),
        check_vma=False,
    )
```

```python
import functools

import jax
import jax.numpy as jnp
from jax import lax
from jax.experimental import pallas as pl
from jax.experimental.pallas import tpu as pltpu
from jax.sharding import PartitionSpec as P

LOG2E = 1.4426950408889634
HEADS = 8
HEAD = 128
TOK = 128
SCALE = HEAD**-0.5
MIB = 2**20
VMEM_MIB = 40
BF16 = jnp.bfloat16
F32 = jnp.float32
VMEM = pl.BlockSpec(memory_space=pltpu.VMEM)
SMEM = pl.BlockSpec(memory_space=pltpu.SMEM)
NT = (((1,), (1,)), ((), ()))
TN = (((0,), (0,)), ((), ()))
NN = (((1,), (0,)), ((), ()))


def dot(a, b, dims):
    return lax.dot_general(a, b, dims, preferred_element_type=F32)


def params(mib):
    return pltpu.CompilerParams(vmem_limit_bytes=mib * MIB)


def shape(dims, dtype=BF16):
    return jax.ShapeDtypeStruct(dims, dtype)


HBM = pl.BlockSpec(memory_space=pltpu.HBM)


QG = 272
ORDER = (4, 3, 5, 2, 6, 1, 7)
SLOT = 528


def lanes_of(head):
    return slice(head * HEAD, (head + 1) * HEAD)


def head_lanes(pos, d):
    head = lax.rem(pos[0] + d, HEADS)
    return pl.ds(pl.multiple_of(head * HEAD, HEAD), HEAD)


def three_parts(row):
    hi = row.astype(BF16).astype(F32)
    rest = row - hi
    mid = rest.astype(BF16).astype(F32)
    return hi, mid, rest - mid


W_PARTS = 12


def pack_heads_body(pos, lse, q, k, v, att, grad, weight, *refs):
    outs, wg_out, refs = refs[:8], refs[8], refs[9:]
    keys, atts, grads, weights, total, low, stats, sem, w_sem, head_sem = refs
    depth = weight.shape[0] // W_PARTS
    first = [
        pltpu.make_async_copy(grad, grads, sem.at[0]),
        pltpu.make_async_copy(att, atts, sem.at[1]),
        pltpu.make_async_copy(k, keys, sem.at[2]),
    ]
    first[0].start()
    w_copies = []
    for i in range(W_PARTS):
        rows = pl.ds(i * depth, depth)
        w_copies.append(pltpu.make_async_copy(weight.at[rows], weights.at[rows], w_sem.at[i]))
        w_copies[i].start()
    first[1].start()
    first[2].start()
    head_copies = []
    for d in range(8):
        lanes = head_lanes(pos, d)
        pairs = ((q, 0), (v, 400))
        for i, (source, row) in enumerate(pairs):
            target = outs[d].at[pl.ds(row, TOK)]
            copy = pltpu.make_async_copy(source.at[:, lanes], target, head_sem.at[i, d])
            copy.start()
            head_copies.append(copy)
    first[0].wait()
    for i in range(W_PARTS):
        rows = slice(i * depth, (i + 1) * depth)
        w_copies[i].wait()
        part = dot(grads[:, rows], weights[rows, :], NN)
        total[...] = part if i == 0 else total[...] + part
    first[1].wait()
    first[2].wait()
    low[...] = total[...].astype(BF16)
    for h in range(HEADS):
        both = low[:, lanes_of(h)].astype(F32) * atts[:, lanes_of(h)].astype(F32)
        stats[h : h + 1, :] = jnp.sum(both.T, axis=0, keepdims=True)
    rows = lax.broadcasted_iota(jnp.int32, (TOK, HEAD), 0)
    valid = rows < TOK - pos[5]
    for d in range(8):
        head = lax.rem(pos[0] + d, HEADS)
        lanes = head_lanes(pos, d)
        parts = three_parts(lse[pl.ds(head, 1), :] * LOG2E) + three_parts(stats[pl.ds(head, 1), :])
        parts = jnp.concatenate(parts + (jnp.zeros((10, TOK), F32),), axis=0)
        outs[d][128:256, :] = low[:, lanes]
        outs[d][256:272, :] = parts.astype(BF16)
        outs[d][272:400, :] = jnp.where(valid, keys[:, lanes].astype(F32), 0.0).astype(BF16)
    for y in range(4):
        for x in range(2):
            at = (x * 4 + y) * 384
            wg_out[y, :, x * 384 : (x + 1) * 384] = grads[:, at : at + 384]
        wg_out[y, :, 768:1792] = atts[...]
    for copy in head_copies:
        copy.wait()


def pack_heads(pos, lse, q, k, v, att, grad, weight):
    return pl.pallas_call(
        pack_heads_body,
        out_shape=(shape((SLOT, 128)),) * 8 + (shape((4, 128, 1792)),),
        in_specs=[SMEM, VMEM] + [HBM] * 6,
        out_specs=(VMEM,) * 9,
        scratch_shapes=[
            pltpu.VMEM(k.shape, BF16),
            pltpu.VMEM(att.shape, BF16),
            pltpu.VMEM(grad.shape, BF16),
            pltpu.VMEM(weight.shape, BF16),
            pltpu.VMEM((128, 1024), F32),
            pltpu.VMEM((128, 1024), BF16),
            pltpu.VMEM((8, 128), F32),
            pltpu.SemaphoreType.DMA((3,)),
            pltpu.SemaphoreType.DMA((W_PARTS,)),
            pltpu.SemaphoreType.DMA((2, HEADS)),
        ],
        compiler_params=params(63),
        cost_estimate=pl.CostEstimate(
            flops=2 * 128 * 3072 * 1024, bytes_accessed=9 * MIB, transcendentals=0
        ),
        name="pack_heads",
    )(pos, lse, q, k, v, att, grad, weight)


def stack_body(*refs):
    slots, (qg, kv) = dict(zip((0,) + ORDER, refs[:8])), refs[8:]
    for d in range(8):
        qg[d] = slots[d][0:QG, :]
        kv[d] = slots[d][QG:SLOT, :]


def stack(slots):
    return pl.pallas_call(
        stack_body,
        out_shape=(shape((8, QG, 128)), shape((8, SLOT - QG, 128))),
        in_specs=[VMEM] * 8,
        out_specs=(VMEM,) * 2,
        compiler_params=params(VMEM_MIB),
        name="stack",
    )(*[slots[d] for d in (0,) + ORDER])


def attend_body(m, n, after, has_acc, has_dq, last_dq, last_acc, *refs):
    refs = list(refs)
    take = lambda count: [refs.pop(0) for _ in range(count)]
    ins = take(m + n + (n if has_acc else 0) + (m if has_dq else 0))
    take(after)
    dq_outs, acc_outs = take(m), take(n)
    qg, kv, acc, dq = take(m), take(n), take(n), take(m)
    dq_low = take(m) if last_dq else None
    acc_low = take(n) if last_acc else None
    in_sem, out_sem = take(2)
    targets = qg + kv + (acc if has_acc else []) + (dq if has_dq else [])
    loads = [
        pltpu.make_async_copy(source, target, in_sem.at[i])
        for i, (source, target) in enumerate(zip(ins, targets))
    ]
    order = [0, m] + [i for i in range(len(ins)) if i not in (0, m)]
    for i in order:
        loads[i].start()
    waited = set()

    def ready(i):
        if i not in waited:
            waited.add(i)
            loads[i].wait()

    stores = []

    def store(source, target):
        copy = pltpu.make_async_copy(source, target, out_sem.at[len(stores)])
        copy.start()
        stores.append(copy)

    for b in range(n):
        for a in range(m):
            ready(a)
            ready(m + b)
            q = qg[a][:, 0:128, :].reshape(1024, 128)
            g = qg[a][:, 128:256, :].reshape(1024, 128)
            rows = [qg[a][j, 256:272, :].astype(F32) for j in range(8)]
            lse = jnp.concatenate([r[0:1] + r[1:2] + r[2:3] for r in rows], axis=1)
            delta = jnp.concatenate([r[3:4] + r[4:5] + r[5:6] for r in rows], axis=1)
            total = None
            for at in range(0, 8, 2):
                span = slice(at, at + 2)
                k = kv[b][span, 0:128, :].reshape(256, 128)
                v = kv[b][span, 128:256, :].reshape(256, 128)
                probs = jnp.exp2(dot(k, q, NT) * (SCALE * LOG2E) - lse)
                moved = (probs * (dot(v, g, NT) - delta)).astype(BF16)
                value_part = dot(probs.astype(BF16), g, NN).reshape(2, 128, 128)
                key_part = dot(moved, q, NN).reshape(2, 128, 128)
                part = dot(k, moved, TN)
                total = part if total is None else total + part
                if has_acc or a > 0:
                    if a == 0 and at == 0:
                        ready(m + n + b)
                    key_part = key_part + acc[b][span, 0:128, :]
                    value_part = value_part + acc[b][span, 128:256, :]
                if last_acc and a == m - 1:
                    acc_low[b][span, 0:128, :] = (key_part * SCALE).astype(BF16)
                    acc_low[b][span, 128:256, :] = value_part.astype(BF16)
                else:
                    acc[b][span, 0:128, :] = key_part
                    acc[b][span, 128:256, :] = value_part
                if a == m - 1:
                    rows = pl.ds(at, 2)
                    store((acc_low[b] if last_acc else acc[b]).at[rows], acc_outs[b].at[rows])
            if has_dq or b > 0:
                if b == 0:
                    ready(m + n + (n if has_acc else 0) + a)
                total = total + dq[a][...]
            if b < n - 1:
                dq[a][...] = total
            elif last_dq:
                dq_low[a][...] = (total.T * SCALE).astype(BF16).reshape(8, 128, 128)
                store(dq_low[a], dq_outs[a])
            else:
                dq[a][...] = total
                store(dq[a], dq_outs[a])
    for copy in stores:
        copy.wait()


def attend(qgs, kvs, accs=None, dqs=None, last_dq=False, last_acc=False, after=()):
    m, n = len(qgs), len(kvs)
    args = list(qgs) + list(kvs) + list(accs or []) + list(dqs or [])
    dq_out = shape((8, 128, 128)) if last_dq else shape((128, 1024), F32)
    acc_out = shape((8, 256, 128), BF16 if last_acc else F32)
    scratch = [pltpu.VMEM((8, QG, 128), BF16)] * m + [pltpu.VMEM((8, 256, 128), BF16)] * n
    scratch += [pltpu.VMEM((8, 256, 128), F32)] * n + [pltpu.VMEM((128, 1024), F32)] * m
    scratch += [pltpu.VMEM((8, 128, 128), BF16)] * (m if last_dq else 0)
    scratch += [pltpu.VMEM((8, 256, 128), BF16)] * (n if last_acc else 0)
    scratch += [pltpu.SemaphoreType.DMA((len(args),)), pltpu.SemaphoreType.DMA((m + 4 * n,))]
    return pl.pallas_call(
        functools.partial(
            attend_body, m, n, len(after), accs is not None, dqs is not None, last_dq, last_acc
        ),
        out_shape=(dq_out,) * m + (acc_out,) * n,
        in_specs=[HBM] * (len(args) + len(after)),
        out_specs=(HBM,) * (m + n),
        scratch_shapes=scratch,
        compiler_params=params(VMEM_MIB),
        cost_estimate=pl.CostEstimate(
            flops=m * n * 20 * 128 * 1024 * 1024,
            bytes_accessed=3 * MIB,
            transcendentals=m * n * 1024 * 1024,
        ),
        name="attend",
    )(*args, *after)


def weight_body(pos, blocks, _, keep, send, total, sorted_rows):
    grad = blocks[:, :, 0:768].reshape(512, 768)
    att = blocks[:, :, 768:1792].reshape(512, 1024)
    for at in range(0, 768, 256):
        total[at : at + 256, :] = dot(grad[:, at : at + 256], att, TN)
    total[768:776, :] = jnp.zeros((8, 1024), F32)
    for x in range(2):
        for z in range(8):
            for lo in range(2):
                for core in range(2):
                    row = x * 384 + ((z * 2 + lo) * 2 + core) * 12
                    rows = total[row : row + 16, :].astype(BF16)
                    sorted_rows[core * 4 + lo * 2 + x, z] = rows
    for i in range(2):
        for j in range(2):
            at = lax.rem(pos[3] + i, 2) * 2 + lax.rem(pos[2] + j, 2)
            keep[i, j] = sorted_rows[pos[4] * 4 + at]
            send[i, j] = sorted_rows[(1 - pos[4]) * 4 + at]


def weight_part(pos, blocks, after):
    return pl.pallas_call(
        weight_body,
        out_shape=(shape((2, 2, 8, 16, 1024)),) * 2,
        in_specs=[SMEM, VMEM, HBM],
        out_specs=(VMEM,) * 2,
        scratch_shapes=[pltpu.VMEM((776, 1024), F32), pltpu.VMEM((8, 8, 16, 1024), BF16)],
        compiler_params=params(VMEM_MIB),
        cost_estimate=pl.CostEstimate(
            flops=2 * 512 * 768 * 1024, bytes_accessed=4 * MIB, transcendentals=0
        ),
        name="weight_part",
    )(pos, blocks, after)


def first_sum_body(keep, came, _, out):
    out[...] = (keep[1].astype(F32) + came[1].astype(F32)).astype(BF16)


def first_sum(keep, came, after):
    return pl.pallas_call(
        first_sum_body,
        out_shape=shape((2, 8, 16, 1024)),
        in_specs=[VMEM, VMEM, HBM],
        out_specs=VMEM,
        compiler_params=params(VMEM_MIB),
        name="first_sum",
    )(keep, came, after)


def second_sum_body(keep, came, came_lo, _, own, send):
    total = keep[0].astype(F32) + came[0].astype(F32) + came_lo[...].astype(F32)
    own[...] = total[0]
    send[...] = total[1].astype(BF16)


def second_sum(keep, came, came_lo, after):
    return pl.pallas_call(
        second_sum_body,
        out_shape=(shape((8, 16, 1024), F32), shape((8, 16, 1024))),
        in_specs=[VMEM, VMEM, VMEM, HBM],
        out_specs=(VMEM, VMEM),
        compiler_params=params(VMEM_MIB),
        name="second_sum",
    )(keep, came, came_lo, after)


def pack_back_body(pos, acc, other, dq, d1, d2, d3, wg, came_hi, *outs):
    own = dq[...].T * SCALE
    for d in range(8):
        rows = slice(d * 128, (d + 1) * 128)
        query = own[rows] + d1[d].astype(F32) + d2[d].astype(F32) + d3[d].astype(F32)
        outs[d][0:128, :] = query.astype(BF16)
        key = acc[d, 0:128, :] * SCALE + other[d, 0:128, :].astype(F32)
        outs[d][128:256, :] = key.astype(BF16)
        value = acc[d, 128:256, :] + other[d, 128:256, :].astype(F32)
        outs[d][256:384, :] = value.astype(BF16)
        block = lax.rem(pos[0] + 8 - d, 8)
        total = (wg[block] + came_hi[block].astype(F32)).astype(BF16)
        for j in range(8):
            outs[d][384 + j * 16 : 400 + j * 16, :] = total[:, j * 128 : (j + 1) * 128]


def pack_back(pos, acc, other, dq, back, wg, came_hi):
    return pl.pallas_call(
        pack_back_body,
        out_shape=(shape((512, 128)),) * 8,
        in_specs=[SMEM] + [VMEM] * 8,
        out_specs=(VMEM,) * 8,
        compiler_params=params(VMEM_MIB),
        name="pack_back",
    )(pos, acc, other, dq, *back, wg, came_hi)


def unpack_body(pos, *refs):
    slots, (gq, gk, gv, wg) = dict(zip((0,) + ORDER, refs[:8])), refs[8:]
    rows = lax.broadcasted_iota(jnp.int32, (TOK, HEAD), 0)
    valid = rows < TOK - pos[5]
    for d in range(8):
        lanes = head_lanes(pos, d)
        gq[:, lanes] = slots[d][0:128, :]
        key = slots[d][128:256, :].astype(F32)
        gk[:, lanes] = jnp.where(valid, key, 0.0).astype(BF16)
        value = slots[d][256:384, :].astype(F32)
        gv[:, lanes] = jnp.where(valid, value, 0.0).astype(BF16)
    for j in range(8):
        span = slice(384 + j * 16, 400 + j * 16)
        total = slots[0][span, :].astype(F32)
        for d in range(1, 8):
            total = total + slots[d][span, :].astype(F32)
        wg[:, j * 128 : (j + 1) * 128] = total[0:12]


def unpack(pos, slots):
    return pl.pallas_call(
        unpack_body,
        out_shape=(shape((128, 1024)),) * 3 + (shape((12, 1024), F32),),
        in_specs=[SMEM] + [VMEM] * 8,
        out_specs=(VMEM,) * 4,
        compiler_params=params(VMEM_MIB),
        name="unpack",
    )(pos, *[slots[d] for d in (0,) + ORDER])


def z_shift(block, distance):
    return lax.ppermute(block, "outer", [(i, (i + distance) % 8) for i in range(8)])


Y_GROUPS = [[0, 1, 2, 3], [4, 5, 6, 7]]


def exchange(slots, sign):
    return [slots[0]] + [z_shift(slots[d], sign * d) for d in range(1, 8)]


def y_shift(block, distance):
    route = [(i, i // 4 * 4 + (i + distance) % 4) for i in range(8)]
    return lax.ppermute(block, "inner", route)


def x_swap(block):
    return lax.ppermute(block, "inner", [(i, (i + 4) % 8) for i in range(8)])


def dp_swap(block, bit):
    return lax.ppermute(block, "dp", [(i, i ^ bit) for i in range(4)])


def on_device(
    queries, key_states, value_states, attention, row_lse, grad_output, out_weight, pad_counts
):
    inner = lax.axis_index("inner")
    dp = lax.axis_index("dp")
    pos = jnp.stack(
        [lax.axis_index("outer"), inner % 4, inner // 4, dp // 2, dp % 2, pad_counts[0, 0]]
    ).astype(jnp.int32)

    packed = pack_heads(
        pos,
        row_lse[0].T,
        queries[0],
        key_states[0],
        value_states[0],
        attention[0],
        grad_output[0],
        out_weight,
    )
    slots = exchange(packed[:8], 1)
    qg, kv = stack(slots)
    qg1, qg3 = y_shift(qg, 1), y_shift(qg, 3)
    kv_far = x_swap(kv)
    qg2 = y_shift(qg1, 1)

    wg_blocks = lax.all_to_all(
        packed[8],
        "inner",
        split_axis=0,
        concat_axis=0,
        axis_index_groups=Y_GROUPS,
        tiled=True,
    )
    keep, send = weight_part(pos, wg_blocks, qg)
    came = dp_swap(send, 1)

    dq0, acc = attend([qg], [kv])
    out_lo = first_sum(keep, came, dq0)
    came_lo = dp_swap(out_lo, 2)
    dq0, far = attend([qg], [kv_far], None, [dq0])
    dq1, dq3, far, acc = attend([qg1, qg3], [kv_far, kv], [far, acc], last_dq=True)
    back1, back3 = y_shift(dq1, 3), y_shift(dq3, 1)
    wg, out_hi = second_sum(keep, came, came_lo, dq1)
    came_hi = x_swap(out_hi)
    dq2, far = attend([qg2], [kv_far], [far], last_acc=True)
    other = x_swap(far)
    dq2, acc = attend([qg2], [kv], [acc], [dq2], last_dq=True)
    back2 = y_shift(dq2, 2)

    back = (back1, back2, back3)
    back_slots = exchange(pack_back(pos, acc, other, dq0, back, wg, came_hi), -1)
    gq, gk, gv, weight_grad = unpack(pos, back_slots)
    return gq[None], gk[None], gv[None], weight_grad


def solution(mesh):
    tokens = P("dp", ("inner", "outer"), None)
    return jax.shard_map(
        on_device,
        mesh=mesh,
        in_specs=(tokens,) * 6 + (P(), P("dp", ("inner", "outer"))),
        out_specs=(tokens,) * 3 + (P(("inner", "outer", "dp"), None),),
        check_vma=False,
    )
```

```python
import functools

import jax
import jax.numpy as jnp
from jax import lax
from jax.experimental import pallas as pl
from jax.experimental.pallas import tpu as pltpu
from jax.sharding import PartitionSpec as P

LOG2E = 1.4426950408889634
HEADS = 8
HEAD = 128
TOK = 128
SCALE = HEAD**-0.5
MIB = 2**20
VMEM_MIB = 40
BF16 = jnp.bfloat16
F32 = jnp.float32
VMEM = pl.BlockSpec(memory_space=pltpu.VMEM)
SMEM = pl.BlockSpec(memory_space=pltpu.SMEM)
NT = (((1,), (1,)), ((), ()))
TN = (((0,), (0,)), ((), ()))
NN = (((1,), (0,)), ((), ()))


def dot(a, b, dims):
    return lax.dot_general(a, b, dims, preferred_element_type=F32)


def params(mib):
    return pltpu.CompilerParams(vmem_limit_bytes=mib * MIB)


def shape(dims, dtype=BF16):
    return jax.ShapeDtypeStruct(dims, dtype)


HBM = pl.BlockSpec(memory_space=pltpu.HBM)


QG = 272
ORDER = (4, 3, 5, 2, 6, 1, 7)
SLOT = 528


def lanes_of(head):
    return slice(head * HEAD, (head + 1) * HEAD)


def head_lanes(pos, d):
    head = lax.rem(pos[0] + d, HEADS)
    return pl.ds(pl.multiple_of(head * HEAD, HEAD), HEAD)


def three_parts(row):
    hi = row.astype(BF16).astype(F32)
    rest = row - hi
    mid = rest.astype(BF16).astype(F32)
    return hi, mid, rest - mid


W_PARTS = 12


def pack_heads_body(pos, lse, q, k, v, att, grad, weight, *refs):
    slots_out, wg_out, refs = refs[:8], refs[8], refs[9:]
    keys, atts, grads, weights, total, low, slots, wg, stats, sem, w_sem, head_sem, out_sem = refs
    depth = weight.shape[0] // W_PARTS
    first = [
        pltpu.make_async_copy(grad, grads, sem.at[0]),
        pltpu.make_async_copy(att, atts, sem.at[1]),
        pltpu.make_async_copy(k, keys, sem.at[2]),
    ]
    for copy in first:
        copy.start()
    w_copies = []
    for i in range(W_PARTS):
        rows = pl.ds(i * depth, depth)
        w_copies.append(pltpu.make_async_copy(weight.at[rows], weights.at[rows], w_sem.at[i]))
        w_copies[i].start()
    head_copies = []
    for d in range(8):
        for i, (source, row) in enumerate(((q, 0), (v, 400))):
            target = slots.at[d, pl.ds(row, TOK)]
            source = source.at[:, head_lanes(pos, d)]
            head_copies.append(pltpu.make_async_copy(source, target, head_sem.at[i, d]))
            head_copies[-1].start()
    out_copies = []

    def send(source, target):
        out_copies.append(pltpu.make_async_copy(source, target, out_sem.at[len(out_copies)]))
        out_copies[-1].start()

    rows = lax.broadcasted_iota(jnp.int32, (TOK, HEAD), 0)
    valid = rows < TOK - pos[5]
    first[0].wait()
    for i in range(W_PARTS):
        rows = slice(i * depth, (i + 1) * depth)
        if i == 1:
            first[1].wait()
        if i == 8:
            first[2].wait()
        w_copies[i].wait()
        if i in (2, 4, 6, 8):
            send(wg.at[i // 2 - 1], wg_out.at[i // 2 - 1])
        part = dot(grads[:, rows], weights[rows, :], NN)
        total[...] = part if i == 0 else total[...] + part
        if i in (1, 3, 5, 7):
            y = i // 2
            for x in range(2):
                at = (x * 4 + y) * 384
                wg[y, :, x * 384 : (x + 1) * 384] = grads[:, at : at + 384]
            wg[y, :, 768:1792] = atts[...]
        if i >= 8:
            for d in (2 * i - 16, 2 * i - 15):
                key = keys[:, head_lanes(pos, d)].astype(F32)
                slots[d, 272:400, :] = jnp.where(valid, key, 0.0).astype(BF16)
    for copy in head_copies:
        copy.wait()
    for d in range(8):
        for row, count in ((0, 128), (272, 256)):
            rows = pl.ds(row, count)
            send(slots.at[d, rows], slots_out[d].at[rows])
    low[...] = total[...].astype(BF16)
    for h in range(HEADS):
        both = low[:, lanes_of(h)].astype(F32) * atts[:, lanes_of(h)].astype(F32)
        stats[h : h + 1, :] = jnp.sum(both.T, axis=0, keepdims=True)
    for d in range(8):
        head = lax.rem(pos[0] + d, HEADS)
        parts = three_parts(lse[pl.ds(head, 1), :] * LOG2E) + three_parts(stats[pl.ds(head, 1), :])
        parts = jnp.concatenate(parts + (jnp.zeros((10, TOK), F32),), axis=0)
        slots[d, 128:256, :] = low[:, head_lanes(pos, d)]
        slots[d, 256:272, :] = parts.astype(BF16)
        rows = pl.ds(128, 144)
        send(slots.at[d, rows], slots_out[d].at[rows])
    for copy in out_copies:
        copy.wait()


def pack_heads(pos, lse, q, k, v, att, grad, weight):
    return pl.pallas_call(
        pack_heads_body,
        out_shape=(shape((SLOT, 128)),) * 8 + (shape((4, 128, 1792)),),
        in_specs=[SMEM, VMEM] + [HBM] * 6,
        out_specs=(HBM,) * 9,
        scratch_shapes=[
            pltpu.VMEM(k.shape, BF16),
            pltpu.VMEM(att.shape, BF16),
            pltpu.VMEM(grad.shape, BF16),
            pltpu.VMEM(weight.shape, BF16),
            pltpu.VMEM((128, 1024), F32),
            pltpu.VMEM((128, 1024), BF16),
            pltpu.VMEM((8, SLOT, 128), BF16),
            pltpu.VMEM((4, 128, 1792), BF16),
            pltpu.VMEM((8, 128), F32),
            pltpu.SemaphoreType.DMA((3,)),
            pltpu.SemaphoreType.DMA((W_PARTS,)),
            pltpu.SemaphoreType.DMA((2, HEADS)),
            pltpu.SemaphoreType.DMA((28,)),
        ],
        compiler_params=params(63),
        cost_estimate=pl.CostEstimate(
            flops=2 * 128 * 3072 * 1024, bytes_accessed=9 * MIB, transcendentals=0
        ),
        name="pack_heads",
    )(pos, lse, q, k, v, att, grad, weight)


def stack_body(*refs):
    slots, (qg, kv) = dict(zip((0,) + ORDER, refs[:8])), refs[8:]
    for d in range(8):
        qg[d] = slots[d][0:QG, :]
        kv[d] = slots[d][QG:SLOT, :]


def stack(slots):
    return pl.pallas_call(
        stack_body,
        out_shape=(shape((8, QG, 128)), shape((8, SLOT - QG, 128))),
        in_specs=[VMEM] * 8,
        out_specs=(VMEM,) * 2,
        compiler_params=params(VMEM_MIB),
        name="stack",
    )(*[slots[d] for d in (0,) + ORDER])


def attend_body(m, n, after, has_acc, has_dq, last_dq, last_acc, *refs):
    refs = list(refs)
    take = lambda count: [refs.pop(0) for _ in range(count)]
    ins = take(m + n + (n if has_acc else 0) + (m if has_dq else 0))
    take(after)
    dq_outs, acc_outs = take(m), take(n)
    qg, kv, acc, dq = take(m), take(n), take(n), take(m)
    dq_low = take(m) if last_dq else None
    acc_low = take(n) if last_acc else None
    in_sem, out_sem = take(2)
    targets = qg + kv + (acc if has_acc else []) + (dq if has_dq else [])
    loads = [
        pltpu.make_async_copy(source, target, in_sem.at[i])
        for i, (source, target) in enumerate(zip(ins, targets))
    ]
    order = [0, m] + [i for i in range(len(ins)) if i not in (0, m)]
    for i in order:
        loads[i].start()
    waited = set()

    def ready(i):
        if i not in waited:
            waited.add(i)
            loads[i].wait()

    stores = []

    def store(source, target):
        copy = pltpu.make_async_copy(source, target, out_sem.at[len(stores)])
        copy.start()
        stores.append(copy)

    for b in range(n):
        for a in range(m):
            ready(a)
            ready(m + b)
            q = qg[a][:, 0:128, :].reshape(1024, 128)
            g = qg[a][:, 128:256, :].reshape(1024, 128)
            rows = [qg[a][j, 256:272, :].astype(F32) for j in range(8)]
            lse = jnp.concatenate([r[0:1] + r[1:2] + r[2:3] for r in rows], axis=1)
            delta = jnp.concatenate([r[3:4] + r[4:5] + r[5:6] for r in rows], axis=1)
            total = None
            for at in range(0, 8, 2):
                span = slice(at, at + 2)
                k = kv[b][span, 0:128, :].reshape(256, 128)
                v = kv[b][span, 128:256, :].reshape(256, 128)
                probs = jnp.exp2(dot(k, q, NT) * (SCALE * LOG2E) - lse)
                moved = (probs * (dot(v, g, NT) - delta)).astype(BF16)
                value_part = dot(probs.astype(BF16), g, NN).reshape(2, 128, 128)
                key_part = dot(moved, q, NN).reshape(2, 128, 128)
                part = dot(k, moved, TN)
                total = part if total is None else total + part
                if has_acc or a > 0:
                    if a == 0 and at == 0:
                        ready(m + n + b)
                    key_part = key_part + acc[b][span, 0:128, :]
                    value_part = value_part + acc[b][span, 128:256, :]
                if last_acc and a == m - 1:
                    acc_low[b][span, 0:128, :] = (key_part * SCALE).astype(BF16)
                    acc_low[b][span, 128:256, :] = value_part.astype(BF16)
                else:
                    acc[b][span, 0:128, :] = key_part
                    acc[b][span, 128:256, :] = value_part
                if a == m - 1:
                    rows = pl.ds(at, 2)
                    store((acc_low[b] if last_acc else acc[b]).at[rows], acc_outs[b].at[rows])
            if has_dq or b > 0:
                if b == 0:
                    ready(m + n + (n if has_acc else 0) + a)
                total = total + dq[a][...]
            if b < n - 1:
                dq[a][...] = total
            elif last_dq:
                dq_low[a][...] = (total.T * SCALE).astype(BF16).reshape(8, 128, 128)
                store(dq_low[a], dq_outs[a])
            else:
                dq[a][...] = total
                store(dq[a], dq_outs[a])
    for copy in stores:
        copy.wait()


def attend(qgs, kvs, accs=None, dqs=None, last_dq=False, last_acc=False, after=()):
    m, n = len(qgs), len(kvs)
    args = list(qgs) + list(kvs) + list(accs or []) + list(dqs or [])
    dq_out = shape((8, 128, 128)) if last_dq else shape((128, 1024), F32)
    acc_out = shape((8, 256, 128), BF16 if last_acc else F32)
    scratch = [pltpu.VMEM((8, QG, 128), BF16)] * m + [pltpu.VMEM((8, 256, 128), BF16)] * n
    scratch += [pltpu.VMEM((8, 256, 128), F32)] * n + [pltpu.VMEM((128, 1024), F32)] * m
    scratch += [pltpu.VMEM((8, 128, 128), BF16)] * (m if last_dq else 0)
    scratch += [pltpu.VMEM((8, 256, 128), BF16)] * (n if last_acc else 0)
    scratch += [pltpu.SemaphoreType.DMA((len(args),)), pltpu.SemaphoreType.DMA((m + 4 * n,))]
    return pl.pallas_call(
        functools.partial(
            attend_body, m, n, len(after), accs is not None, dqs is not None, last_dq, last_acc
        ),
        out_shape=(dq_out,) * m + (acc_out,) * n,
        in_specs=[HBM] * (len(args) + len(after)),
        out_specs=(HBM,) * (m + n),
        scratch_shapes=scratch,
        compiler_params=params(VMEM_MIB),
        cost_estimate=pl.CostEstimate(
            flops=m * n * 20 * 128 * 1024 * 1024,
            bytes_accessed=3 * MIB,
            transcendentals=m * n * 1024 * 1024,
        ),
        name="attend",
    )(*args, *after)


def weight_body(pos, blocks, _, keep, send, total, sorted_rows):
    grad = blocks[:, :, 0:768].reshape(512, 768)
    att = blocks[:, :, 768:1792].reshape(512, 1024)
    for at in range(0, 768, 256):
        total[at : at + 256, :] = dot(grad[:, at : at + 256], att, TN)
    total[768:776, :] = jnp.zeros((8, 1024), F32)
    for x in range(2):
        for z in range(8):
            for lo in range(2):
                for core in range(2):
                    row = x * 384 + ((z * 2 + lo) * 2 + core) * 12
                    rows = total[row : row + 16, :].astype(BF16)
                    sorted_rows[core * 4 + lo * 2 + x, z] = rows
    for i in range(2):
        for j in range(2):
            at = lax.rem(pos[3] + i, 2) * 2 + lax.rem(pos[2] + j, 2)
            keep[i, j] = sorted_rows[pos[4] * 4 + at]
            send[i, j] = sorted_rows[(1 - pos[4]) * 4 + at]


def weight_part(pos, blocks, after):
    return pl.pallas_call(
        weight_body,
        out_shape=(shape((2, 2, 8, 16, 1024)),) * 2,
        in_specs=[SMEM, VMEM, HBM],
        out_specs=(VMEM,) * 2,
        scratch_shapes=[pltpu.VMEM((776, 1024), F32), pltpu.VMEM((8, 8, 16, 1024), BF16)],
        compiler_params=params(VMEM_MIB),
        cost_estimate=pl.CostEstimate(
            flops=2 * 512 * 768 * 1024, bytes_accessed=4 * MIB, transcendentals=0
        ),
        name="weight_part",
    )(pos, blocks, after)


def first_sum_body(keep, came, _, out):
    out[...] = (keep[1].astype(F32) + came[1].astype(F32)).astype(BF16)


def first_sum(keep, came, after):
    return pl.pallas_call(
        first_sum_body,
        out_shape=shape((2, 8, 16, 1024)),
        in_specs=[VMEM, VMEM, HBM],
        out_specs=VMEM,
        compiler_params=params(VMEM_MIB),
        name="first_sum",
    )(keep, came, after)


def second_sum_body(keep, came, came_lo, _, own, send):
    total = keep[0].astype(F32) + came[0].astype(F32) + came_lo[...].astype(F32)
    own[...] = total[0]
    send[...] = total[1].astype(BF16)


def second_sum(keep, came, came_lo, after):
    return pl.pallas_call(
        second_sum_body,
        out_shape=(shape((8, 16, 1024), F32), shape((8, 16, 1024))),
        in_specs=[VMEM, VMEM, VMEM, HBM],
        out_specs=(VMEM, VMEM),
        compiler_params=params(VMEM_MIB),
        name="second_sum",
    )(keep, came, came_lo, after)


def pack_back_body(pos, acc, other, dq, d1, d2, d3, wg, came_hi, *outs):
    own = dq[...].T * SCALE
    for d in range(8):
        rows = slice(d * 128, (d + 1) * 128)
        query = own[rows] + d1[d].astype(F32) + d2[d].astype(F32) + d3[d].astype(F32)
        outs[d][0:128, :] = query.astype(BF16)
        both = acc[d].astype(F32) + other[d].astype(F32)
        outs[d][128:384, :] = both.astype(BF16)
        block = lax.rem(pos[0] + 8 - d, 8)
        total = wg[block] + came_hi[block].astype(F32)
        for row, count, at in ((0, 8, 384), (8, 4, 448)):
            parts = [total[row : row + count, lanes_of(j)] for j in range(8)]
            parts = jnp.concatenate(parts, axis=0).astype(BF16)
            outs[d][at : at + count * 8, :] = parts


def pack_back(pos, acc, other, dq, back, wg, came_hi):
    return pl.pallas_call(
        pack_back_body,
        out_shape=(shape((480, 128)),) * 8,
        in_specs=[SMEM] + [VMEM] * 8,
        out_specs=(VMEM,) * 8,
        compiler_params=params(VMEM_MIB),
        name="pack_back",
    )(pos, acc, other, dq, *back, wg, came_hi)


def unpack_body(pos, *refs):
    slots, (gq, gk, gv, wg) = dict(zip((0,) + ORDER, refs[:8])), refs[8:]
    rows = lax.broadcasted_iota(jnp.int32, (TOK, HEAD), 0)
    valid = rows < TOK - pos[5]
    for d in range(8):
        lanes = head_lanes(pos, d)
        gq[:, lanes] = slots[d][0:128, :]
        key = slots[d][128:256, :].astype(F32)
        gk[:, lanes] = jnp.where(valid, key, 0.0).astype(BF16)
        value = slots[d][256:384, :].astype(F32)
        gv[:, lanes] = jnp.where(valid, value, 0.0).astype(BF16)
    total = slots[0][384:480, :].astype(F32)
    for d in range(1, 8):
        total = total + slots[d][384:480, :].astype(F32)
    for j in range(8):
        wg[0:8, lanes_of(j)] = total[j * 8 : j * 8 + 8]
        wg[8:12, lanes_of(j)] = total[64 + j * 4 : 68 + j * 4]


def unpack(pos, slots):
    return pl.pallas_call(
        unpack_body,
        out_shape=(shape((128, 1024)),) * 3 + (shape((12, 1024), F32),),
        in_specs=[SMEM] + [VMEM] * 8,
        out_specs=(VMEM,) * 4,
        compiler_params=params(VMEM_MIB),
        name="unpack",
    )(pos, *[slots[d] for d in (0,) + ORDER])


def z_shift(block, distance):
    return lax.ppermute(block, "outer", [(i, (i + distance) % 8) for i in range(8)])


Y_GROUPS = [[0, 1, 2, 3], [4, 5, 6, 7]]


def exchange(slots, sign):
    return [slots[0]] + [z_shift(slots[d], sign * d) for d in range(1, 8)]


def y_shift(block, distance):
    route = [(i, i // 4 * 4 + (i + distance) % 4) for i in range(8)]
    return lax.ppermute(block, "inner", route)


def x_swap(block):
    return lax.ppermute(block, "inner", [(i, (i + 4) % 8) for i in range(8)])


def dp_swap(block, bit):
    return lax.ppermute(block, "dp", [(i, i ^ bit) for i in range(4)])


def on_device(
    queries, key_states, value_states, attention, row_lse, grad_output, out_weight, pad_counts
):
    inner = lax.axis_index("inner")
    dp = lax.axis_index("dp")
    pos = jnp.stack(
        [lax.axis_index("outer"), inner % 4, inner // 4, dp // 2, dp % 2, pad_counts[0, 0]]
    ).astype(jnp.int32)

    packed = pack_heads(
        pos,
        row_lse[0].T,
        queries[0],
        key_states[0],
        value_states[0],
        attention[0],
        grad_output[0],
        out_weight,
    )
    slots = exchange(packed[:8], 1)
    qg, kv = stack(slots)
    qg1, qg3 = y_shift(qg, 1), y_shift(qg, 3)
    kv_far = x_swap(kv)
    qg2 = y_shift(qg1, 1)

    wg_blocks = lax.all_to_all(
        packed[8],
        "inner",
        split_axis=0,
        concat_axis=0,
        axis_index_groups=Y_GROUPS,
        tiled=True,
    )
    keep, send = weight_part(pos, wg_blocks, qg)
    came = dp_swap(send, 1)

    dq0, acc = attend([qg], [kv])
    out_lo = first_sum(keep, came, dq0)
    came_lo = dp_swap(out_lo, 2)
    dq0, far = attend([qg], [kv_far], None, [dq0])
    dq1, dq3, far, acc = attend([qg1, qg3], [kv_far, kv], [far, acc], last_dq=True)
    back1, back3 = y_shift(dq1, 3), y_shift(dq3, 1)
    wg, out_hi = second_sum(keep, came, came_lo, dq1)
    came_hi = x_swap(out_hi)
    dq2, far = attend([qg2], [kv_far], [far], last_acc=True)
    other = x_swap(far)
    dq2, acc = attend([qg2], [kv], [acc], [dq2], last_dq=True, last_acc=True, after=[came_hi])
    back2 = y_shift(dq2, 2)

    back = (back1, back2, back3)
    back_slots = exchange(pack_back(pos, acc, other, dq0, back, wg, came_hi), -1)
    gq, gk, gv, weight_grad = unpack(pos, back_slots)
    return gq[None], gk[None], gv[None], weight_grad


def solution(mesh):
    tokens = P("dp", ("inner", "outer"), None)
    return jax.shard_map(
        on_device,
        mesh=mesh,
        in_specs=(tokens,) * 6 + (P(), P("dp", ("inner", "outer"))),
        out_specs=(tokens,) * 3 + (P(("inner", "outer", "dp"), None),),
        check_vma=False,
    )
```

```python
import functools

import jax
import jax.numpy as jnp
from jax import lax
from jax.experimental import pallas as pl
from jax.experimental.pallas import tpu as pltpu
from jax.sharding import PartitionSpec as P

LOG2E = 1.4426950408889634
HEADS = 8
HEAD = 128
TOK = 128
SCALE = HEAD**-0.5
MIB = 2**20
VMEM_MIB = 40
BF16 = jnp.bfloat16
F32 = jnp.float32
VMEM = pl.BlockSpec(memory_space=pltpu.VMEM)
SMEM = pl.BlockSpec(memory_space=pltpu.SMEM)
NT = (((1,), (1,)), ((), ()))
TN = (((0,), (0,)), ((), ()))
NN = (((1,), (0,)), ((), ()))


def dot(a, b, dims):
    return lax.dot_general(a, b, dims, preferred_element_type=F32)


def params(mib):
    return pltpu.CompilerParams(vmem_limit_bytes=mib * MIB)


def shape(dims, dtype=BF16):
    return jax.ShapeDtypeStruct(dims, dtype)


HBM = pl.BlockSpec(memory_space=pltpu.HBM)


QG = 272
ORDER = (4, 3, 5, 2, 6, 1, 7)
SLOT = 528


def lanes_of(head):
    return slice(head * HEAD, (head + 1) * HEAD)


def head_lanes(pos, d):
    head = lax.rem(pos[0] + d, HEADS)
    return pl.ds(pl.multiple_of(head * HEAD, HEAD), HEAD)


def three_parts(row):
    hi = row.astype(BF16).astype(F32)
    rest = row - hi
    mid = rest.astype(BF16).astype(F32)
    return hi, mid, rest - mid


W_PARTS = 4


def pack_heads_body(pos, lse, q, k, v, att, grad, weight, *refs):
    slots_out, wg_out, refs = refs[:8], refs[8], refs[9:]
    qs, ks, vs, atts, grads, weights, total, low, slots, wg, stats, sem, w_sem, out_sem = refs
    depth = weight.shape[0] // W_PARTS
    first = [
        pltpu.make_async_copy(source, target, sem.at[i])
        for i, (source, target) in enumerate(
            ((grad, grads), (att, atts), (q, qs), (k, ks), (v, vs))
        )
    ]
    first[0].start()
    w_copies = []
    for i in range(W_PARTS):
        rows = pl.ds(i * depth, depth)
        w_copies.append(pltpu.make_async_copy(weight.at[rows], weights.at[rows], w_sem.at[i]))
        w_copies[i].start()
        first[i + 1].start()
    out_copies = []

    def send(source, target):
        out_copies.append(pltpu.make_async_copy(source, target, out_sem.at[len(out_copies)]))
        out_copies[-1].start()

    rows = lax.broadcasted_iota(jnp.int32, (TOK, HEAD), 0)
    valid = rows < TOK - pos[5]
    first[0].wait()
    for i in range(W_PARTS):
        rows = slice(i * depth, (i + 1) * depth)
        w_copies[i].wait()
        first[i + 1].wait()
        part = dot(grads[:, rows], weights[rows, :], NN)
        total[...] = part if i == 0 else total[...] + part
        for x in range(2):
            at = (x * 4 + i) * 384
            wg[i, :, x * 384 : (x + 1) * 384] = grads[:, at : at + 384]
        wg[i, :, 768:1792] = atts[...]
        send(wg.at[i], wg_out.at[i])
        for d in range(8):
            lanes = head_lanes(pos, d)
            if i == 1:
                slots[d, 0:128, :] = qs[:, lanes]
            if i == 2:
                key = jnp.where(valid, ks[:, lanes].astype(F32), 0.0)
                slots[d, 272:400, :] = key.astype(BF16)
            if i == 3:
                slots[d, 400:528, :] = vs[:, lanes]
    low[...] = total[...].astype(BF16)
    for h in range(HEADS):
        both = low[:, lanes_of(h)].astype(F32) * atts[:, lanes_of(h)].astype(F32)
        stats[h : h + 1, :] = jnp.sum(both.T, axis=0, keepdims=True)
    for d in range(8):
        head = lax.rem(pos[0] + d, HEADS)
        parts = three_parts(lse[pl.ds(head, 1), :] * LOG2E) + three_parts(stats[pl.ds(head, 1), :])
        parts = jnp.concatenate(parts + (jnp.zeros((10, TOK), F32),), axis=0)
        slots[d, 128:256, :] = low[:, head_lanes(pos, d)]
        slots[d, 256:272, :] = parts.astype(BF16)
        send(slots.at[d], slots_out[d])
    for copy in out_copies:
        copy.wait()


def pack_heads(pos, lse, q, k, v, att, grad, weight):
    return pl.pallas_call(
        pack_heads_body,
        out_shape=(shape((SLOT, 128)),) * 8 + (shape((4, 128, 1792)),),
        in_specs=[SMEM, VMEM] + [HBM] * 6,
        out_specs=(HBM,) * 9,
        scratch_shapes=[
            pltpu.VMEM(q.shape, BF16),
            pltpu.VMEM(k.shape, BF16),
            pltpu.VMEM(v.shape, BF16),
            pltpu.VMEM(att.shape, BF16),
            pltpu.VMEM(grad.shape, BF16),
            pltpu.VMEM(weight.shape, BF16),
            pltpu.VMEM((128, 1024), F32),
            pltpu.VMEM((128, 1024), BF16),
            pltpu.VMEM((8, SLOT, 128), BF16),
            pltpu.VMEM((4, 128, 1792), BF16),
            pltpu.VMEM((8, 128), F32),
            pltpu.SemaphoreType.DMA((5,)),
            pltpu.SemaphoreType.DMA((W_PARTS,)),
            pltpu.SemaphoreType.DMA((12,)),
        ],
        compiler_params=params(63),
        cost_estimate=pl.CostEstimate(
            flops=2 * 128 * 3072 * 1024, bytes_accessed=9 * MIB, transcendentals=0
        ),
        name="pack_heads",
    )(pos, lse, q, k, v, att, grad, weight)


def stack_body(*refs):
    slots, (qg, kv) = dict(zip((0,) + ORDER, refs[:8])), refs[8:]
    for d in range(8):
        qg[d] = slots[d][0:QG, :]
        kv[d] = slots[d][QG:SLOT, :]


def stack(slots):
    return pl.pallas_call(
        stack_body,
        out_shape=(shape((8, QG, 128)), shape((8, SLOT - QG, 128))),
        in_specs=[VMEM] * 8,
        out_specs=(VMEM,) * 2,
        compiler_params=params(VMEM_MIB),
        name="stack",
    )(*[slots[d] for d in (0,) + ORDER])


def attend_body(m, n, after, has_acc, has_dq, last_dq, last_acc, *refs):
    refs = list(refs)
    take = lambda count: [refs.pop(0) for _ in range(count)]
    ins = take(m + n + (n if has_acc else 0) + (m if has_dq else 0))
    take(after)
    dq_outs, acc_outs = take(m), take(n)
    qg, kv, acc, dq = take(m), take(n), take(n), take(m)
    dq_low = take(m) if last_dq else None
    acc_low = take(n) if last_acc else None
    in_sem, out_sem = take(2)
    targets = qg + kv + (acc if has_acc else []) + (dq if has_dq else [])
    loads = [
        pltpu.make_async_copy(source, target, in_sem.at[i])
        for i, (source, target) in enumerate(zip(ins, targets))
    ]
    order = [0, m] + [i for i in range(len(ins)) if i not in (0, m)]
    for i in order:
        loads[i].start()
    waited = set()

    def ready(i):
        if i not in waited:
            waited.add(i)
            loads[i].wait()

    stores = []

    def store(source, target):
        copy = pltpu.make_async_copy(source, target, out_sem.at[len(stores)])
        copy.start()
        stores.append(copy)

    for b in range(n):
        for a in range(m):
            ready(a)
            ready(m + b)
            q = qg[a][:, 0:128, :].reshape(1024, 128)
            g = qg[a][:, 128:256, :].reshape(1024, 128)
            rows = [qg[a][j, 256:272, :].astype(F32) for j in range(8)]
            lse = jnp.concatenate([r[0:1] + r[1:2] + r[2:3] for r in rows], axis=1)
            delta = jnp.concatenate([r[3:4] + r[4:5] + r[5:6] for r in rows], axis=1)
            total = None
            for at in range(0, 8, 2):
                span = slice(at, at + 2)
                k = kv[b][span, 0:128, :].reshape(256, 128)
                v = kv[b][span, 128:256, :].reshape(256, 128)
                probs = jnp.exp2(dot(k, q, NT) * (SCALE * LOG2E) - lse)
                moved = (probs * (dot(v, g, NT) - delta)).astype(BF16)
                value_part = dot(probs.astype(BF16), g, NN).reshape(2, 128, 128)
                key_part = dot(moved, q, NN).reshape(2, 128, 128)
                part = dot(k, moved, TN)
                total = part if total is None else total + part
                if has_acc or a > 0:
                    if a == 0 and at == 0:
                        ready(m + n + b)
                    key_part = key_part + acc[b][span, 0:128, :]
                    value_part = value_part + acc[b][span, 128:256, :]
                if last_acc and a == m - 1:
                    acc_low[b][span, 0:128, :] = (key_part * SCALE).astype(BF16)
                    acc_low[b][span, 128:256, :] = value_part.astype(BF16)
                else:
                    acc[b][span, 0:128, :] = key_part
                    acc[b][span, 128:256, :] = value_part
                if a == m - 1:
                    rows = pl.ds(at, 2)
                    store((acc_low[b] if last_acc else acc[b]).at[rows], acc_outs[b].at[rows])
            if has_dq or b > 0:
                if b == 0:
                    ready(m + n + (n if has_acc else 0) + a)
                total = total + dq[a][...]
            if b < n - 1:
                dq[a][...] = total
            elif last_dq:
                dq_low[a][...] = (total.T * SCALE).astype(BF16).reshape(8, 128, 128)
                store(dq_low[a], dq_outs[a])
            else:
                dq[a][...] = total
                store(dq[a], dq_outs[a])
    for copy in stores:
        copy.wait()


def attend(qgs, kvs, accs=None, dqs=None, last_dq=False, last_acc=False, after=()):
    m, n = len(qgs), len(kvs)
    args = list(qgs) + list(kvs) + list(accs or []) + list(dqs or [])
    dq_out = shape((8, 128, 128)) if last_dq else shape((128, 1024), F32)
    acc_out = shape((8, 256, 128), BF16 if last_acc else F32)
    scratch = [pltpu.VMEM((8, QG, 128), BF16)] * m + [pltpu.VMEM((8, 256, 128), BF16)] * n
    scratch += [pltpu.VMEM((8, 256, 128), F32)] * n + [pltpu.VMEM((128, 1024), F32)] * m
    scratch += [pltpu.VMEM((8, 128, 128), BF16)] * (m if last_dq else 0)
    scratch += [pltpu.VMEM((8, 256, 128), BF16)] * (n if last_acc else 0)
    scratch += [pltpu.SemaphoreType.DMA((len(args),)), pltpu.SemaphoreType.DMA((m + 4 * n,))]
    return pl.pallas_call(
        functools.partial(
            attend_body, m, n, len(after), accs is not None, dqs is not None, last_dq, last_acc
        ),
        out_shape=(dq_out,) * m + (acc_out,) * n,
        in_specs=[HBM] * (len(args) + len(after)),
        out_specs=(HBM,) * (m + n),
        scratch_shapes=scratch,
        compiler_params=params(VMEM_MIB),
        cost_estimate=pl.CostEstimate(
            flops=m * n * 20 * 128 * 1024 * 1024,
            bytes_accessed=3 * MIB,
            transcendentals=m * n * 1024 * 1024,
        ),
        name="attend",
    )(*args, *after)


def weight_body(pos, blocks, _, keep, send, total, sorted_rows):
    grad = blocks[:, :, 0:768].reshape(512, 768)
    att = blocks[:, :, 768:1792].reshape(512, 1024)
    for at in range(0, 768, 256):
        total[at : at + 256, :] = dot(grad[:, at : at + 256], att, TN)
    total[768:776, :] = jnp.zeros((8, 1024), F32)
    for x in range(2):
        for z in range(8):
            for lo in range(2):
                for core in range(2):
                    row = x * 384 + ((z * 2 + lo) * 2 + core) * 12
                    rows = total[row : row + 16, :].astype(BF16)
                    sorted_rows[core * 4 + lo * 2 + x, z] = rows
    for i in range(2):
        for j in range(2):
            at = lax.rem(pos[3] + i, 2) * 2 + lax.rem(pos[2] + j, 2)
            keep[i, j] = sorted_rows[pos[4] * 4 + at]
            send[i, j] = sorted_rows[(1 - pos[4]) * 4 + at]


def weight_part(pos, blocks, after):
    return pl.pallas_call(
        weight_body,
        out_shape=(shape((2, 2, 8, 16, 1024)),) * 2,
        in_specs=[SMEM, VMEM, HBM],
        out_specs=(VMEM,) * 2,
        scratch_shapes=[pltpu.VMEM((776, 1024), F32), pltpu.VMEM((8, 8, 16, 1024), BF16)],
        compiler_params=params(VMEM_MIB),
        cost_estimate=pl.CostEstimate(
            flops=2 * 512 * 768 * 1024, bytes_accessed=4 * MIB, transcendentals=0
        ),
        name="weight_part",
    )(pos, blocks, after)


def first_sum_body(keep, came, _, out):
    out[...] = (keep[1].astype(F32) + came[1].astype(F32)).astype(BF16)


def first_sum(keep, came, after):
    return pl.pallas_call(
        first_sum_body,
        out_shape=shape((2, 8, 16, 1024)),
        in_specs=[VMEM, VMEM, HBM],
        out_specs=VMEM,
        compiler_params=params(VMEM_MIB),
        name="first_sum",
    )(keep, came, after)


def second_sum_body(keep, came, came_lo, _, own, send):
    total = keep[0].astype(F32) + came[0].astype(F32) + came_lo[...].astype(F32)
    own[...] = total[0]
    send[...] = total[1].astype(BF16)


def second_sum(keep, came, came_lo, after):
    return pl.pallas_call(
        second_sum_body,
        out_shape=(shape((8, 16, 1024), F32), shape((8, 16, 1024))),
        in_specs=[VMEM, VMEM, VMEM, HBM],
        out_specs=(VMEM, VMEM),
        compiler_params=params(VMEM_MIB),
        name="second_sum",
    )(keep, came, came_lo, after)


def pack_back_body(pos, acc, other, dq, d1, d2, d3, wg, came_hi, *outs):
    own = dq[...].T * SCALE
    for d in range(8):
        rows = slice(d * 128, (d + 1) * 128)
        query = own[rows] + d1[d].astype(F32) + d2[d].astype(F32) + d3[d].astype(F32)
        outs[d][0:128, :] = query.astype(BF16)
        both = acc[d].astype(F32) + other[d].astype(F32)
        outs[d][128:384, :] = both.astype(BF16)
        block = lax.rem(pos[0] + 8 - d, 8)
        total = wg[block] + came_hi[block].astype(F32)
        for row, count, at in ((0, 8, 384), (8, 4, 448)):
            parts = [total[row : row + count, lanes_of(j)] for j in range(8)]
            parts = jnp.concatenate(parts, axis=0).astype(BF16)
            outs[d][at : at + count * 8, :] = parts


def pack_back(pos, acc, other, dq, back, wg, came_hi):
    return pl.pallas_call(
        pack_back_body,
        out_shape=(shape((480, 128)),) * 8,
        in_specs=[SMEM] + [VMEM] * 8,
        out_specs=(VMEM,) * 8,
        compiler_params=params(VMEM_MIB),
        name="pack_back",
    )(pos, acc, other, dq, *back, wg, came_hi)


def unpack_body(pos, *refs):
    slots, (gq, gk, gv, wg) = dict(zip((0,) + ORDER, refs[:8])), refs[8:]
    rows = lax.broadcasted_iota(jnp.int32, (TOK, HEAD), 0)
    valid = rows < TOK - pos[5]
    for d in range(8):
        lanes = head_lanes(pos, d)
        gq[:, lanes] = slots[d][0:128, :]
        key = slots[d][128:256, :].astype(F32)
        gk[:, lanes] = jnp.where(valid, key, 0.0).astype(BF16)
        value = slots[d][256:384, :].astype(F32)
        gv[:, lanes] = jnp.where(valid, value, 0.0).astype(BF16)
    total = slots[0][384:480, :].astype(F32)
    for d in range(1, 8):
        total = total + slots[d][384:480, :].astype(F32)
    for j in range(8):
        wg[0:8, lanes_of(j)] = total[j * 8 : j * 8 + 8]
        wg[8:12, lanes_of(j)] = total[64 + j * 4 : 68 + j * 4]


def unpack(pos, slots):
    return pl.pallas_call(
        unpack_body,
        out_shape=(shape((128, 1024)),) * 3 + (shape((12, 1024), F32),),
        in_specs=[SMEM] + [VMEM] * 8,
        out_specs=(VMEM,) * 4,
        compiler_params=params(VMEM_MIB),
        name="unpack",
    )(pos, *[slots[d] for d in (0,) + ORDER])


def z_shift(block, distance):
    return lax.ppermute(block, "outer", [(i, (i + distance) % 8) for i in range(8)])


Y_GROUPS = [[0, 1, 2, 3], [4, 5, 6, 7]]


def exchange(slots, sign):
    return [slots[0]] + [z_shift(slots[d], sign * d) for d in range(1, 8)]


def y_shift(block, distance):
    route = [(i, i // 4 * 4 + (i + distance) % 4) for i in range(8)]
    return lax.ppermute(block, "inner", route)


def x_swap(block):
    return lax.ppermute(block, "inner", [(i, (i + 4) % 8) for i in range(8)])


def dp_swap(block, bit):
    return lax.ppermute(block, "dp", [(i, i ^ bit) for i in range(4)])


def on_device(
    queries, key_states, value_states, attention, row_lse, grad_output, out_weight, pad_counts
):
    inner = lax.axis_index("inner")
    dp = lax.axis_index("dp")
    pos = jnp.stack(
        [lax.axis_index("outer"), inner % 4, inner // 4, dp // 2, dp % 2, pad_counts[0, 0]]
    ).astype(jnp.int32)

    packed = pack_heads(
        pos,
        row_lse[0].T,
        queries[0],
        key_states[0],
        value_states[0],
        attention[0],
        grad_output[0],
        out_weight,
    )
    slots = exchange(packed[:8], 1)
    qg, kv = stack(slots)
    qg1, qg3 = y_shift(qg, 1), y_shift(qg, 3)
    kv_far = x_swap(kv)
    qg2 = y_shift(qg1, 1)

    wg_blocks = lax.all_to_all(
        packed[8],
        "inner",
        split_axis=0,
        concat_axis=0,
        axis_index_groups=Y_GROUPS,
        tiled=True,
    )
    keep, send = weight_part(pos, wg_blocks, qg)
    came = dp_swap(send, 1)

    dq0, acc = attend([qg], [kv])
    out_lo = first_sum(keep, came, dq0)
    came_lo = dp_swap(out_lo, 2)
    dq0, far = attend([qg], [kv_far], None, [dq0])
    dq1, dq3, far, acc = attend([qg1, qg3], [kv_far, kv], [far, acc], last_dq=True)
    back1, back3 = y_shift(dq1, 3), y_shift(dq3, 1)
    wg, out_hi = second_sum(keep, came, came_lo, dq1)
    came_hi = x_swap(out_hi)
    dq2, far = attend([qg2], [kv_far], [far], last_acc=True)
    other = x_swap(far)
    dq2, acc = attend([qg2], [kv], [acc], [dq2], last_dq=True, last_acc=True, after=[came_hi])
    back2 = y_shift(dq2, 2)

    back = (back1, back2, back3)
    back_slots = exchange(pack_back(pos, acc, other, dq0, back, wg, came_hi), -1)
    gq, gk, gv, weight_grad = unpack(pos, back_slots)
    return gq[None], gk[None], gv[None], weight_grad


def solution(mesh):
    tokens = P("dp", ("inner", "outer"), None)
    return jax.shard_map(
        on_device,
        mesh=mesh,
        in_specs=(tokens,) * 6 + (P(), P("dp", ("inner", "outer"))),
        out_specs=(tokens,) * 3 + (P(("inner", "outer", "dp"), None),),
        check_vma=False,
    )
```

```python
import functools

import jax
import jax.numpy as jnp
from jax import lax
from jax.experimental import pallas as pl
from jax.experimental.pallas import tpu as pltpu
from jax.sharding import PartitionSpec as P

LOG2E = 1.4426950408889634
HEADS = 8
HEAD = 128
TOK = 128
SCALE = HEAD**-0.5
MIB = 2**20
VMEM_MIB = 40
BF16 = jnp.bfloat16
F32 = jnp.float32
VMEM = pl.BlockSpec(memory_space=pltpu.VMEM)
SMEM = pl.BlockSpec(memory_space=pltpu.SMEM)
NT = (((1,), (1,)), ((), ()))
TN = (((0,), (0,)), ((), ()))
NN = (((1,), (0,)), ((), ()))


def dot(a, b, dims):
    return lax.dot_general(a, b, dims, preferred_element_type=F32)


def params(mib):
    return pltpu.CompilerParams(vmem_limit_bytes=mib * MIB)


def shape(dims, dtype=BF16):
    return jax.ShapeDtypeStruct(dims, dtype)


HBM = pl.BlockSpec(memory_space=pltpu.HBM)


QG = 272
ORDER = (4, 3, 5, 2, 6, 1, 7)
SLOT = 528


def lanes_of(head):
    return slice(head * HEAD, (head + 1) * HEAD)


def head_lanes(pos, d):
    head = lax.rem(pos[0] + d, HEADS)
    return pl.ds(pl.multiple_of(head * HEAD, HEAD), HEAD)


def three_parts(row):
    hi = row.astype(BF16).astype(F32)
    rest = row - hi
    mid = rest.astype(BF16).astype(F32)
    return hi, mid, rest - mid


W_PARTS = 4


def pack_heads_body(pos, lse, q, k, v, att, grad, weight, *refs):
    slots_out, wg_out, refs = refs[:8], refs[8], refs[9:]
    qs, ks, vs, atts, grads, weights, total, low, slots, wg, stats, sem, w_sem, out_sem = refs
    depth = weight.shape[0] // W_PARTS
    first = [
        pltpu.make_async_copy(source, target, sem.at[i])
        for i, (source, target) in enumerate(
            ((grad, grads), (att, atts), (q, qs), (k, ks), (v, vs))
        )
    ]
    first[0].start()
    w_copies = []
    for i in range(W_PARTS):
        rows = pl.ds(i * depth, depth)
        w_copies.append(pltpu.make_async_copy(weight.at[rows], weights.at[rows], w_sem.at[i]))
        w_copies[i].start()
        first[i + 1].start()
    out_copies = []

    def send(source, target):
        out_copies.append(pltpu.make_async_copy(source, target, out_sem.at[len(out_copies)]))
        out_copies[-1].start()

    rows = lax.broadcasted_iota(jnp.int32, (TOK, HEAD), 0)
    valid = rows < TOK - pos[5]
    first[0].wait()
    for i in range(W_PARTS):
        rows = slice(i * depth, (i + 1) * depth)
        w_copies[i].wait()
        first[i + 1].wait()
        part = dot(grads[:, rows], weights[rows, :], NN)
        total[...] = part if i == 0 else total[...] + part
        for x in range(2):
            at = (x * 4 + i) * 384
            wg[i, :, x * 384 : (x + 1) * 384] = grads[:, at : at + 384]
        wg[i, :, 768:1792] = atts[...]
        send(wg.at[i], wg_out.at[i])
        for d in range(8):
            lanes = head_lanes(pos, d)
            if i == 1:
                slots[d, 0:128, :] = qs[:, lanes]
            if i == 2:
                key = jnp.where(valid, ks[:, lanes].astype(F32), 0.0)
                slots[d, 272:400, :] = key.astype(BF16)
            if i == 3:
                slots[d, 400:528, :] = vs[:, lanes]
    low[...] = total[...].astype(BF16)
    for h in range(HEADS):
        both = low[:, lanes_of(h)].astype(F32) * atts[:, lanes_of(h)].astype(F32)
        stats[h : h + 1, :] = jnp.sum(both.T, axis=0, keepdims=True)
    for d in range(8):
        head = lax.rem(pos[0] + d, HEADS)
        parts = three_parts(lse[pl.ds(head, 1), :] * LOG2E) + three_parts(stats[pl.ds(head, 1), :])
        parts = jnp.concatenate(parts + (jnp.zeros((10, TOK), F32),), axis=0)
        slots[d, 128:256, :] = low[:, head_lanes(pos, d)]
        slots[d, 256:272, :] = parts.astype(BF16)
        send(slots.at[d], slots_out[d])
    for copy in out_copies:
        copy.wait()


def pack_heads(pos, lse, q, k, v, att, grad, weight):
    return pl.pallas_call(
        pack_heads_body,
        out_shape=(shape((SLOT, 128)),) * 8 + (shape((4, 128, 1792)),),
        in_specs=[SMEM, VMEM] + [HBM] * 6,
        out_specs=(HBM,) * 9,
        scratch_shapes=[
            pltpu.VMEM(q.shape, BF16),
            pltpu.VMEM(k.shape, BF16),
            pltpu.VMEM(v.shape, BF16),
            pltpu.VMEM(att.shape, BF16),
            pltpu.VMEM(grad.shape, BF16),
            pltpu.VMEM(weight.shape, BF16),
            pltpu.VMEM((128, 1024), F32),
            pltpu.VMEM((128, 1024), BF16),
            pltpu.VMEM((8, SLOT, 128), BF16),
            pltpu.VMEM((4, 128, 1792), BF16),
            pltpu.VMEM((8, 128), F32),
            pltpu.SemaphoreType.DMA((5,)),
            pltpu.SemaphoreType.DMA((W_PARTS,)),
            pltpu.SemaphoreType.DMA((12,)),
        ],
        compiler_params=params(63),
        cost_estimate=pl.CostEstimate(
            flops=2 * 128 * 3072 * 1024, bytes_accessed=9 * MIB, transcendentals=0
        ),
        name="pack_heads",
    )(pos, lse, q, k, v, att, grad, weight)


def stack_body(*refs):
    slots, (qg, kv) = dict(zip((0,) + ORDER, refs[:8])), refs[8:]
    for d in range(8):
        qg[d] = slots[d][0:QG, :]
        kv[d] = slots[d][QG:SLOT, :]


def stack(slots):
    return pl.pallas_call(
        stack_body,
        out_shape=(shape((8, QG, 128)), shape((8, SLOT - QG, 128))),
        in_specs=[VMEM] * 8,
        out_specs=(VMEM,) * 2,
        compiler_params=params(VMEM_MIB),
        name="stack",
    )(*[slots[d] for d in (0,) + ORDER])


def attend_body(m, n, after, has_acc, has_dq, last_dq, last_acc, *refs):
    refs = list(refs)
    take = lambda count: [refs.pop(0) for _ in range(count)]
    ins = take(m + n + (n if has_acc else 0) + (m if has_dq else 0))
    take(after)
    dq_outs, acc_outs = take(m), take(n)
    qg, kv, acc, dq = take(m), take(n), take(n), take(m)
    dq_low = take(m) if last_dq else None
    acc_low = take(n) if last_acc else None
    in_sem, out_sem = take(2)
    targets = qg + kv + (acc if has_acc else []) + (dq if has_dq else [])
    loads = [
        pltpu.make_async_copy(source, target, in_sem.at[i])
        for i, (source, target) in enumerate(zip(ins, targets))
    ]
    order = [0, m] + [i for i in range(len(ins)) if i not in (0, m)]
    for i in order:
        loads[i].start()
    waited = set()

    def ready(i):
        if i not in waited:
            waited.add(i)
            loads[i].wait()

    stores = []

    def store(source, target):
        copy = pltpu.make_async_copy(source, target, out_sem.at[len(stores)])
        copy.start()
        stores.append(copy)

    for b in range(n):
        for a in range(m):
            ready(a)
            ready(m + b)
            q = qg[a][:, 0:128, :].reshape(1024, 128)
            g = qg[a][:, 128:256, :].reshape(1024, 128)
            rows = [qg[a][j, 256:272, :].astype(F32) for j in range(8)]
            lse = jnp.concatenate([r[0:1] + r[1:2] + r[2:3] for r in rows], axis=1)
            delta = jnp.concatenate([r[3:4] + r[4:5] + r[5:6] for r in rows], axis=1)
            total = None
            for at in range(0, 8, 2):
                span = slice(at, at + 2)
                k = kv[b][span, 0:128, :].reshape(256, 128)
                v = kv[b][span, 128:256, :].reshape(256, 128)
                probs = jnp.exp2(dot(k, q, NT) * (SCALE * LOG2E) - lse)
                moved = (probs * (dot(v, g, NT) - delta)).astype(BF16)
                value_part = dot(probs.astype(BF16), g, NN).reshape(2, 128, 128)
                key_part = dot(moved, q, NN).reshape(2, 128, 128)
                part = dot(k, moved, TN)
                total = part if total is None else total + part
                if has_acc or a > 0:
                    if a == 0 and at == 0:
                        ready(m + n + b)
                    key_part = key_part + acc[b][span, 0:128, :]
                    value_part = value_part + acc[b][span, 128:256, :]
                if last_acc and a == m - 1:
                    acc_low[b][span, 0:128, :] = (key_part * SCALE).astype(BF16)
                    acc_low[b][span, 128:256, :] = value_part.astype(BF16)
                else:
                    acc[b][span, 0:128, :] = key_part
                    acc[b][span, 128:256, :] = value_part
                if a == m - 1:
                    rows = pl.ds(at, 2)
                    store((acc_low[b] if last_acc else acc[b]).at[rows], acc_outs[b].at[rows])
            if has_dq or b > 0:
                if b == 0:
                    ready(m + n + (n if has_acc else 0) + a)
                total = total + dq[a][...]
            if b < n - 1:
                dq[a][...] = total
            elif last_dq:
                for at in range(0, 8, 2):
                    part = total[:, at * 128 : (at + 2) * 128].T * SCALE
                    dq_low[a][at : at + 2] = part.astype(BF16).reshape(2, 128, 128)
                    rows = pl.ds(at, 2)
                    store(dq_low[a].at[rows], dq_outs[a].at[rows])
            else:
                dq[a][...] = total
                store(dq[a], dq_outs[a])
    for copy in stores:
        copy.wait()


def attend(qgs, kvs, accs=None, dqs=None, last_dq=False, last_acc=False, after=()):
    m, n = len(qgs), len(kvs)
    args = list(qgs) + list(kvs) + list(accs or []) + list(dqs or [])
    dq_out = shape((8, 128, 128)) if last_dq else shape((128, 1024), F32)
    acc_out = shape((8, 256, 128), BF16 if last_acc else F32)
    scratch = [pltpu.VMEM((8, QG, 128), BF16)] * m + [pltpu.VMEM((8, 256, 128), BF16)] * n
    scratch += [pltpu.VMEM((8, 256, 128), F32)] * n + [pltpu.VMEM((128, 1024), F32)] * m
    scratch += [pltpu.VMEM((8, 128, 128), BF16)] * (m if last_dq else 0)
    scratch += [pltpu.VMEM((8, 256, 128), BF16)] * (n if last_acc else 0)
    scratch += [pltpu.SemaphoreType.DMA((len(args),)), pltpu.SemaphoreType.DMA((4 * m + 4 * n,))]
    return pl.pallas_call(
        functools.partial(
            attend_body, m, n, len(after), accs is not None, dqs is not None, last_dq, last_acc
        ),
        out_shape=(dq_out,) * m + (acc_out,) * n,
        in_specs=[HBM] * (len(args) + len(after)),
        out_specs=(HBM,) * (m + n),
        scratch_shapes=scratch,
        compiler_params=params(VMEM_MIB),
        cost_estimate=pl.CostEstimate(
            flops=m * n * 20 * 128 * 1024 * 1024,
            bytes_accessed=3 * MIB,
            transcendentals=m * n * 1024 * 1024,
        ),
        name="attend",
    )(*args, *after)


def weight_body(pos, blocks, _, keep, send, total, sorted_rows):
    grad = blocks[:, :, 0:768].reshape(512, 768)
    att = blocks[:, :, 768:1792].reshape(512, 1024)
    for at in range(0, 768, 256):
        total[at : at + 256, :] = dot(grad[:, at : at + 256], att, TN)
    total[768:776, :] = jnp.zeros((8, 1024), F32)
    for x in range(2):
        for z in range(8):
            for lo in range(2):
                for core in range(2):
                    row = x * 384 + ((z * 2 + lo) * 2 + core) * 12
                    rows = total[row : row + 16, :].astype(BF16)
                    sorted_rows[core * 4 + lo * 2 + x, z] = rows
    for i in range(2):
        for j in range(2):
            at = lax.rem(pos[3] + i, 2) * 2 + lax.rem(pos[2] + j, 2)
            keep[i, j] = sorted_rows[pos[4] * 4 + at]
            send[i, j] = sorted_rows[(1 - pos[4]) * 4 + at]


def weight_part(pos, blocks, after):
    return pl.pallas_call(
        weight_body,
        out_shape=(shape((2, 2, 8, 16, 1024)),) * 2,
        in_specs=[SMEM, VMEM, HBM],
        out_specs=(VMEM,) * 2,
        scratch_shapes=[pltpu.VMEM((776, 1024), F32), pltpu.VMEM((8, 8, 16, 1024), BF16)],
        compiler_params=params(VMEM_MIB),
        cost_estimate=pl.CostEstimate(
            flops=2 * 512 * 768 * 1024, bytes_accessed=4 * MIB, transcendentals=0
        ),
        name="weight_part",
    )(pos, blocks, after)


def first_sum_body(keep, came, _, out):
    out[...] = (keep[1].astype(F32) + came[1].astype(F32)).astype(BF16)


def first_sum(keep, came, after):
    return pl.pallas_call(
        first_sum_body,
        out_shape=shape((2, 8, 16, 1024)),
        in_specs=[VMEM, VMEM, HBM],
        out_specs=VMEM,
        compiler_params=params(VMEM_MIB),
        name="first_sum",
    )(keep, came, after)


def second_sum_body(keep, came, came_lo, _, own, send):
    total = keep[0].astype(F32) + came[0].astype(F32) + came_lo[...].astype(F32)
    own[...] = total[0]
    send[...] = total[1].astype(BF16)


def second_sum(keep, came, came_lo, after):
    return pl.pallas_call(
        second_sum_body,
        out_shape=(shape((8, 16, 1024), F32), shape((8, 16, 1024))),
        in_specs=[VMEM, VMEM, VMEM, HBM],
        out_specs=(VMEM, VMEM),
        compiler_params=params(VMEM_MIB),
        name="second_sum",
    )(keep, came, came_lo, after)


def pack_back_body(pos, acc, other, dq, d1, d2, d3, wg, came_hi, *outs):
    own = dq[...].T * SCALE
    for d in range(8):
        rows = slice(d * 128, (d + 1) * 128)
        query = own[rows] + d1[d].astype(F32) + d2[d].astype(F32) + d3[d].astype(F32)
        outs[d][0:128, :] = query.astype(BF16)
        both = acc[d].astype(F32) + other[d].astype(F32)
        outs[d][128:384, :] = both.astype(BF16)
        block = lax.rem(pos[0] + 8 - d, 8)
        total = wg[block] + came_hi[block].astype(F32)
        for row, count, at in ((0, 8, 384), (8, 4, 448)):
            parts = [total[row : row + count, lanes_of(j)] for j in range(8)]
            parts = jnp.concatenate(parts, axis=0).astype(BF16)
            outs[d][at : at + count * 8, :] = parts


def pack_back(pos, acc, other, dq, back, wg, came_hi):
    return pl.pallas_call(
        pack_back_body,
        out_shape=(shape((480, 128)),) * 8,
        in_specs=[SMEM] + [VMEM] * 8,
        out_specs=(VMEM,) * 8,
        compiler_params=params(VMEM_MIB),
        name="pack_back",
    )(pos, acc, other, dq, *back, wg, came_hi)


def unpack_body(pos, *refs):
    slots, (gq, gk, gv, wg) = dict(zip((0,) + ORDER, refs[:8])), refs[8:]
    rows = lax.broadcasted_iota(jnp.int32, (TOK, HEAD), 0)
    valid = rows < TOK - pos[5]
    for d in range(8):
        lanes = head_lanes(pos, d)
        gq[:, lanes] = slots[d][0:128, :]
        key = slots[d][128:256, :].astype(F32)
        gk[:, lanes] = jnp.where(valid, key, 0.0).astype(BF16)
        value = slots[d][256:384, :].astype(F32)
        gv[:, lanes] = jnp.where(valid, value, 0.0).astype(BF16)
    total = slots[0][384:480, :].astype(F32)
    for d in range(1, 8):
        total = total + slots[d][384:480, :].astype(F32)
    for j in range(8):
        wg[0:8, lanes_of(j)] = total[j * 8 : j * 8 + 8]
        wg[8:12, lanes_of(j)] = total[64 + j * 4 : 68 + j * 4]


def unpack(pos, slots):
    return pl.pallas_call(
        unpack_body,
        out_shape=(shape((128, 1024)),) * 3 + (shape((12, 1024), F32),),
        in_specs=[SMEM] + [VMEM] * 8,
        out_specs=(VMEM,) * 4,
        compiler_params=params(VMEM_MIB),
        name="unpack",
    )(pos, *[slots[d] for d in (0,) + ORDER])


def z_shift(block, distance):
    return lax.ppermute(block, "outer", [(i, (i + distance) % 8) for i in range(8)])


Y_GROUPS = [[0, 1, 2, 3], [4, 5, 6, 7]]


def exchange(slots, sign):
    return [slots[0]] + [z_shift(slots[d], sign * d) for d in range(1, 8)]


def y_shift(block, distance):
    route = [(i, i // 4 * 4 + (i + distance) % 4) for i in range(8)]
    return lax.ppermute(block, "inner", route)


def x_swap(block):
    return lax.ppermute(block, "inner", [(i, (i + 4) % 8) for i in range(8)])


def dp_swap(block, bit):
    return lax.ppermute(block, "dp", [(i, i ^ bit) for i in range(4)])


def on_device(
    queries, key_states, value_states, attention, row_lse, grad_output, out_weight, pad_counts
):
    inner = lax.axis_index("inner")
    dp = lax.axis_index("dp")
    pos = jnp.stack(
        [lax.axis_index("outer"), inner % 4, inner // 4, dp // 2, dp % 2, pad_counts[0, 0]]
    ).astype(jnp.int32)

    packed = pack_heads(
        pos,
        row_lse[0].T,
        queries[0],
        key_states[0],
        value_states[0],
        attention[0],
        grad_output[0],
        out_weight,
    )
    slots = exchange(packed[:8], 1)
    qg, kv = stack(slots)
    qg1, qg3 = y_shift(qg, 1), y_shift(qg, 3)
    kv_far = x_swap(kv)
    qg2 = y_shift(qg1, 1)

    wg_blocks = lax.all_to_all(
        packed[8],
        "inner",
        split_axis=0,
        concat_axis=0,
        axis_index_groups=Y_GROUPS,
        tiled=True,
    )
    keep, send = weight_part(pos, wg_blocks, qg)
    came = dp_swap(send, 1)

    dq0, acc = attend([qg], [kv])
    out_lo = first_sum(keep, came, dq0)
    came_lo = dp_swap(out_lo, 2)
    dq0, far = attend([qg], [kv_far], None, [dq0])
    dq1, dq3, far, acc = attend([qg1, qg3], [kv_far, kv], [far, acc], last_dq=True)
    back1, back3 = y_shift(dq1, 3), y_shift(dq3, 1)
    wg, out_hi = second_sum(keep, came, came_lo, dq1)
    came_hi = x_swap(out_hi)
    dq2, far = attend([qg2], [kv_far], [far], last_acc=True)
    other = x_swap(far)
    dq2, acc = attend([qg2], [kv], [acc], [dq2], last_dq=True, last_acc=True, after=[came_hi])
    back2 = y_shift(dq2, 2)

    back = (back1, back2, back3)
    back_slots = exchange(pack_back(pos, acc, other, dq0, back, wg, came_hi), -1)
    gq, gk, gv, weight_grad = unpack(pos, back_slots)
    return gq[None], gk[None], gv[None], weight_grad


def solution(mesh):
    tokens = P("dp", ("inner", "outer"), None)
    return jax.shard_map(
        on_device,
        mesh=mesh,
        in_specs=(tokens,) * 6 + (P(), P("dp", ("inner", "outer"))),
        out_specs=(tokens,) * 3 + (P(("inner", "outer", "dp"), None),),
        check_vma=False,
    )
```
